32 devices in a mesh: groups: 2 (over y), ctx: 16 (over z, x, core).
Axes of the slice: x: 2, y: 2, z: 4, core: 2. Of those that a mesh axis runs over, the one named last changes fastest.
Arguments:
- values: bfloat16 [2048, 4096], P(None, ('groups', 'ctx')), parts along dimension 1, may hold values from -6 to 6
- keys: bfloat16 [2048, 4096], P(None, ('groups', 'ctx')), parts along dimension 1, may hold values from -6 to 6
- queries: bfloat16 [2048, 4096], P(None, ('groups', 'ctx')), parts along dimension 1, may hold values from -6 to 6
- grad_out: bfloat16 [2048, 4096], P(None, ('groups', 'ctx')), parts along dimension 1, may hold values from -6 to 6
- filters: float32 [2048, 2048], P(None, 'ctx'), may hold values from -4 to 4, as said below
Outputs:
- grad_values: bfloat16 [2048, 4096], P(None, ('groups', 'ctx')), parts along dimension 1
- grad_keys: bfloat16 [2048, 4096], P(None, ('groups', 'ctx')), parts along dimension 1
- grad_queries: bfloat16 [2048, 4096], P(None, ('groups', 'ctx')), parts along dimension 1
- grad_filters: float32 [2048, 4096], P(None, ('groups', 'ctx')), parts along dimension 1
The draws below stay inside these ranges and needn't reach their ends.
There are 2 independent parts, one for each index of `groups`. The reference program is written for one: setup_inputs(seed, part) draws one part's arguments, and reference() takes and returns one part's arrays. A program takes and returns all parts, laid end to end along the dimension named above; an argument that names none is the same for every part. Nothing has to cross between parts.
Inputs may be any that keep to these rules, and one draw needn't show every extreme that they name: `filters`: each channel's filter decays along its taps at a rate of its own.
All inputs are finite; a program needn't handle non-finite values.
Results may differ from the reference program's by a relative error of at most 0.0092.
Values may be sent and summed in bfloat16 or wider, within the bound.
No kernel may reach another device: no remote copies, remote signals or barrier semaphores. Data moves between devices by JAX's collectives and lax.ppermute only.
A program may use at most 64 MiB of HBM per device.

```python
import math
import jax
import jax.numpy as jnp
from jax import lax

D = 2048
LEN = 2048
LONG = 256
SHORT = 16


def draw_filters(key, part):
    key = jax.random.fold_in(key, 7)
    rate_key, noise_key = jax.random.split(key)
    rate = jnp.exp(jax.random.uniform(rate_key, (D, 1), jnp.float32, jnp.log(0.3), jnp.log(30.0)))
    noise = jnp.clip(jax.random.normal(noise_key, (D, LEN), jnp.float32), -4.0, 4.0)
    taps = jnp.arange(LEN, dtype=jnp.float32)[None, :] / LEN
    sigma = jnp.sqrt((1.0 - jnp.exp(-2.0 * rate / LEN)) / (1.0 - jnp.exp(-2.0 * rate)))
    return noise * sigma * jnp.exp(-rate * taps)


def level_of(rng, extent, cuts, low, high):
    level, own = 1.0, jax.random.fold_in(rng, 6)
    for position, parts in cuts:
        draws = jnp.exp(jax.random.uniform(jax.random.fold_in(own, position), (parts,), jnp.float32, low / len(cuts), high / len(cuts)))
        level = level * jnp.repeat(draws, extent[position] // parts).reshape([-1 if axis == position else 1 for axis in range(len(extent))])
    return level


def bell_draw(rng, extent, spread, most, shards=(), held_as=jnp.bfloat16):
    gain = level_of(rng, extent, shards, -0.22, 0.18) if shards else 1.0
    entries = jax.random.normal(rng, extent, jnp.float32) * spread * gain
    return jnp.minimum(jnp.maximum(entries, -most), most).astype(held_as)


def setup_inputs(seed: int = 0, part: int = 0) -> dict:
    key_of = jax.random.split(jax.random.key(seed), 6)
    part_splits = jax.random.split(jax.random.fold_in(key_of[5], part), 6)
    values = bell_draw(part_splits[0], (D, LEN), 1.0, 6.0, ((1, 16),))
    keys = bell_draw(part_splits[1], (D, LEN), 1.0, 6.0, ((1, 16),))
    queries = bell_draw(part_splits[2], (D, LEN), 1.0, 6.0, ((1, 16),))
    grad_out = bell_draw(part_splits[3], (D, LEN), 1.0, 6.0, ((1, 16),))
    filters = draw_filters(jax.random.fold_in(key_of[5], 71), part)
    return dict(values=values, keys=keys, queries=queries, grad_out=grad_out, filters=filters)


def dft_tables(long_side, short_side):
    full_len = long_side * short_side
    short_idx = jnp.arange(short_side, dtype=jnp.int32)
    long_idx = jnp.arange(long_side, dtype=jnp.int32)
    short_ang = (jnp.outer(short_idx, short_idx) % short_side).astype(jnp.float32) * (-2.0 * math.pi / short_side)
    long_ang = (jnp.outer(long_idx, long_idx) % long_side).astype(jnp.float32) * (-2.0 * math.pi / long_side)
    twist_ang = (jnp.outer(short_idx, long_idx) % full_len).astype(jnp.float32) * (-2.0 * math.pi / full_len)
    return (jnp.cos(short_ang).astype(jnp.bfloat16), jnp.sin(short_ang).astype(jnp.bfloat16),
            jnp.cos(long_ang).astype(jnp.bfloat16), jnp.sin(long_ang).astype(jnp.bfloat16),
            jnp.cos(twist_ang), jnp.sin(twist_ang))


def product(pattern, left, right):
    return jnp.einsum(pattern, left.astype(jnp.float32), right.astype(jnp.float32), precision=lax.Precision.HIGHEST)


def forward(signal, tables):
    small_re, small_im, large_re, large_im, twist_re, twist_im = tables
    channels = signal.shape[0]
    short_side = small_re.shape[0]
    long_side = large_re.shape[0]
    padded = jnp.concatenate([signal, jnp.zeros_like(signal)], axis=1).reshape(channels, short_side, long_side)
    section_re = product('kn,cnp->ckp', small_re, padded)
    section_im = product('kn,cnp->ckp', small_im, padded)
    turned_re = (section_re * twist_re - section_im * twist_im).astype(jnp.bfloat16)
    turned_im = (section_re * twist_im + section_im * twist_re).astype(jnp.bfloat16)
    spec_re = product('ckp,pj->ckj', turned_re, large_re) - product('ckp,pj->ckj', turned_im, large_im)
    spec_im = product('ckp,pj->ckj', turned_re, large_im) + product('ckp,pj->ckj', turned_im, large_re)
    return spec_re, spec_im


def inverse(spec_re, spec_im, tables):
    small_re, small_im, large_re, large_im, twist_re, twist_im = tables
    channels, short_side, long_side = spec_re.shape
    full_len = short_side * long_side
    round_re = spec_re.astype(jnp.bfloat16)
    round_im = spec_im.astype(jnp.bfloat16)
    back_re = product('ckj,jp->ckp', round_re, large_re) + product('ckj,jp->ckp', round_im, large_im)
    back_im = product('ckj,jp->ckp', round_im, large_re) - product('ckj,jp->ckp', round_re, large_im)
    turned_re = (back_re * twist_re + back_im * twist_im).astype(jnp.bfloat16)
    turned_im = (back_im * twist_re - back_re * twist_im).astype(jnp.bfloat16)
    signal = product('nk,ckp->cnp', small_re, turned_re) + product('nk,ckp->cnp', small_im, turned_im)
    return signal.reshape(channels, full_len)[:, :full_len // 2] / full_len


def block_grads(values, keys, queries, grad_out, filters, tables):
    mixed = (values.astype(jnp.float32) * keys.astype(jnp.float32)).astype(jnp.bfloat16)
    grad_conv = (grad_out.astype(jnp.float32) * queries.astype(jnp.float32)).astype(jnp.bfloat16)
    mix_re, mix_im = forward(mixed, tables)
    fil_re, fil_im = forward(filters.astype(jnp.bfloat16), tables)
    grd_re, grd_im = forward(grad_conv, tables)
    conv_out = inverse(fil_re * mix_re - fil_im * mix_im, fil_re * mix_im + fil_im * mix_re, tables).astype(jnp.bfloat16)
    grad_mixed = inverse(fil_re * grd_re + fil_im * grd_im, fil_re * grd_im - fil_im * grd_re, tables).astype(jnp.bfloat16)
    grad_filters = inverse(grd_re * mix_re + grd_im * mix_im, grd_im * mix_re - grd_re * mix_im, tables)
    grad_wide = grad_mixed.astype(jnp.float32)
    grad_queries = (grad_out.astype(jnp.float32) * conv_out.astype(jnp.float32)).astype(jnp.bfloat16)
    grad_keys = (grad_wide * values.astype(jnp.float32)).astype(jnp.bfloat16)
    grad_values = (grad_wide * keys.astype(jnp.float32)).astype(jnp.bfloat16)
    return grad_values, grad_keys, grad_queries, grad_filters


def reference(values, keys, queries, grad_out, filters):
    block_size = 32
    tables = dft_tables(LONG, SHORT)
    blocks = D // block_size

    def split_rows(array):
        return array.reshape(blocks, block_size, LEN)

    def per_block(items):
        return block_grads(items[0], items[1], items[2], items[3], items[4], tables)

    results = lax.map(per_block, (split_rows(values), split_rows(keys), split_rows(queries), split_rows(grad_out), split_rows(filters)))
    grad_values, grad_keys, grad_queries, grad_filters = results
    return (grad_values.reshape(D, LEN), grad_keys.reshape(D, LEN), grad_queries.reshape(D, LEN), grad_filters.reshape(D, LEN))
```

```python
import math

import jax
import jax.numpy as jnp
from jax import lax
from jax.sharding import PartitionSpec as P


def dft_tables(long_side, short_side):
    full_len = long_side * short_side
    short_idx = jnp.arange(short_side, dtype=jnp.int32)
    long_idx = jnp.arange(long_side, dtype=jnp.int32)
    short_ang = (jnp.outer(short_idx, short_idx) % short_side).astype(jnp.float32) * (
        -2.0 * math.pi / short_side
    )
    long_ang = (jnp.outer(long_idx, long_idx) % long_side).astype(jnp.float32) * (
        -2.0 * math.pi / long_side
    )
    twist_ang = (jnp.outer(short_idx, long_idx) % full_len).astype(jnp.float32) * (
        -2.0 * math.pi / full_len
    )
    return (
        jnp.cos(short_ang).astype(jnp.bfloat16),
        jnp.sin(short_ang).astype(jnp.bfloat16),
        jnp.cos(long_ang).astype(jnp.bfloat16),
        jnp.sin(long_ang).astype(jnp.bfloat16),
        jnp.cos(twist_ang),
        jnp.sin(twist_ang),
    )


def product(pattern, left, right):
    return jnp.einsum(pattern, left, right, preferred_element_type=jnp.float32)


def forward(signal, tables):
    small_re, small_im, large_re, large_im, twist_re, twist_im = tables
    channels = signal.shape[0]
    short_side = small_re.shape[0]
    long_side = large_re.shape[0]
    padded = jnp.concatenate([signal, jnp.zeros_like(signal)], axis=1).reshape(
        channels, short_side, long_side
    )
    section_re = product("kn,cnp->ckp", small_re, padded)
    section_im = product("kn,cnp->ckp", small_im, padded)
    turned_re = (section_re * twist_re - section_im * twist_im).astype(jnp.bfloat16)
    turned_im = (section_re * twist_im + section_im * twist_re).astype(jnp.bfloat16)
    spec_re = product("ckp,pj->ckj", turned_re, large_re) - product(
        "ckp,pj->ckj", turned_im, large_im
    )
    spec_im = product("ckp,pj->ckj", turned_re, large_im) + product(
        "ckp,pj->ckj", turned_im, large_re
    )
    return (spec_re, spec_im)


def inverse(spec_re, spec_im, tables):
    small_re, small_im, large_re, large_im, twist_re, twist_im = tables
    channels, short_side, long_side = spec_re.shape
    full_len = short_side * long_side
    round_re = spec_re.astype(jnp.bfloat16)
    round_im = spec_im.astype(jnp.bfloat16)
    back_re = product("ckj,jp->ckp", round_re, large_re) + product(
        "ckj,jp->ckp", round_im, large_im
    )
    back_im = product("ckj,jp->ckp", round_im, large_re) - product(
        "ckj,jp->ckp", round_re, large_im
    )
    turned_re = (back_re * twist_re + back_im * twist_im).astype(jnp.bfloat16)
    turned_im = (back_im * twist_re - back_re * twist_im).astype(jnp.bfloat16)
    signal = product("nk,ckp->cnp", small_re, turned_re) + product(
        "nk,ckp->cnp", small_im, turned_im
    )
    return signal.reshape(channels, full_len)[:, : full_len // 2] / full_len


def gate_mul(left, right):
    return (left.astype(jnp.float32) * right.astype(jnp.float32)).astype(jnp.bfloat16)


def shards(values, keys, queries, grad_out, filters):
    ctx_count = lax.axis_size("ctx")
    tok_rows = values.shape[1]
    tables = dft_tables(2 * tok_rows, ctx_count)
    grad_conv, mixed, filter_chan = (
        lax.all_to_all(gate_mul(grad_out, queries), "ctx", split_axis=0, concat_axis=1, tiled=True),
        lax.all_to_all(gate_mul(values, keys), "ctx", split_axis=0, concat_axis=1, tiled=True),
        lax.all_to_all(
            filters.astype(jnp.bfloat16), "ctx", split_axis=0, concat_axis=1, tiled=True
        ),
    )
    mix_re, mix_im = forward(mixed, tables)
    fil_re, fil_im = forward(filter_chan, tables)
    grd_re, grd_im = forward(grad_conv, tables)
    conv_out = inverse(
        fil_re * mix_re - fil_im * mix_im, fil_re * mix_im + fil_im * mix_re, tables
    ).astype(jnp.bfloat16)
    grad_mixed = inverse(
        fil_re * grd_re + fil_im * grd_im, fil_re * grd_im - fil_im * grd_re, tables
    ).astype(jnp.bfloat16)
    grad_filt = inverse(
        grd_re * mix_re + grd_im * mix_im, grd_im * mix_re - grd_re * mix_im, tables
    )
    conv_tok, mixed_tok, filter_tok = (
        lax.all_to_all(conv_out, "ctx", split_axis=1, concat_axis=0, tiled=True),
        lax.all_to_all(grad_mixed, "ctx", split_axis=1, concat_axis=0, tiled=True),
        lax.all_to_all(
            grad_filt.astype(jnp.bfloat16), "ctx", split_axis=1, concat_axis=0, tiled=True
        ).astype(grad_filt.dtype),
    )
    return (
        gate_mul(mixed_tok, keys),
        gate_mul(mixed_tok, values),
        gate_mul(grad_out, conv_tok),
        filter_tok,
    )


def solution(mesh):
    return jax.shard_map(
        shards,
        mesh=mesh,
        in_specs=(
            P(None, ("groups", "ctx")),
            P(None, ("groups", "ctx")),
            P(None, ("groups", "ctx")),
            P(None, ("groups", "ctx")),
            P(None, "ctx"),
        ),
        out_specs=(
            P(None, ("groups", "ctx")),
            P(None, ("groups", "ctx")),
            P(None, ("groups", "ctx")),
            P(None, ("groups", "ctx")),
        ),
        check_vma=False,
    )
```

```python
import math

import jax
import jax.numpy as jnp
import numpy as np
from jax import lax
from jax.experimental import pallas as pl
from jax.experimental.pallas import tpu as pltpu
from jax.sharding import PartitionSpec as P

TILE = 16


def leaf_angles(count, theta=math.pi / 2):
    if count == 1:
        return [theta]
    half = theta / 2
    return leaf_angles(count // 2, half) + leaf_angles(count // 2, half + math.pi)


def evaluate(points, theta):
    count = len(points)
    if count == 1:
        return points
    half, phi = count // 2, theta / 2
    c, s = math.cos(phi), math.sin(phi)
    first, second = [], []
    for low, high in zip(points[:half], points[half:]):
        if low[1] is None:
            turned_re, turned_im = high[0] * c, high[0] * -s
            first.append((low[0] + turned_re, turned_im))
            second.append((low[0] - turned_re, -turned_im))
        else:
            turned_re = high[0] * c + high[1] * s
            turned_im = high[1] * c - high[0] * s
            first.append((low[0] + turned_re, low[1] + turned_im))
            second.append((low[0] - turned_re, low[1] - turned_im))
    return evaluate(first, phi) + evaluate(second, phi + math.pi)


def interpolate(values, theta, top=True):
    count = len(values)
    if count == 1:
        return values
    half, phi = count // 2, theta / 2
    c, s = math.cos(phi), math.sin(phi)
    first = interpolate(values[:half], phi, False)
    second = interpolate(values[half:], phi + math.pi, False)
    low, high = [], []
    for (a_re, a_im), (b_re, b_im) in zip(first, second):
        gap_re, gap_im = a_re - b_re, a_im - b_im
        if top:
            low.append(a_re + b_re)
            high.append(gap_re * c - gap_im * s)
        else:
            low.append((a_re + b_re, a_im + b_im))
            high.append((gap_re * c - gap_im * s, gap_re * s + gap_im * c))
    return low + high


def make_tables(shards, width):
    angles = np.array(leaf_angles(shards))
    turn = np.outer(angles, np.arange(width)) / width
    scale = 1.0 / (shards * width)
    twist = np.stack(
        [np.cos(turn), np.sin(turn), np.cos(turn) * scale, np.sin(turn) * scale], axis=1
    ).astype(np.float32)
    wave = np.outer(np.arange(width), np.arange(width)) % width * (2 * math.pi / width)
    c, s = np.cos(wave), np.sin(wave)
    ahead = np.block([[c, -s], [s, c]])
    return twist, jnp.asarray(ahead, jnp.bfloat16), jnp.asarray(ahead.T, jnp.bfloat16)


def gate_kernel(value_ref, key_ref, query_ref, cot_ref, filter_ref, out_ref):
    out_ref[0, 0] = (
        value_ref[...].astype(jnp.float32) * key_ref[...].astype(jnp.float32)
    ).astype(jnp.bfloat16)
    out_ref[0, 1] = (
        cot_ref[...].astype(jnp.float32) * query_ref[...].astype(jnp.float32)
    ).astype(jnp.bfloat16)
    out_ref[0, 2] = filter_ref[...].astype(jnp.bfloat16)


def spectral_kernel(sig_ref, twist_ref, ahead_ref, back_ref, out_ref, turned_ref):
    shards, _, tile, width = sig_ref.shape
    specs = []
    for which in range(3):
        points = [(sig_ref[b, which].astype(jnp.float32), None) for b in range(shards)]
        for k, (re, im) in enumerate(evaluate(points, math.pi / 2)):
            c, s = twist_ref[k, 0:1, :], twist_ref[k, 1:2, :]
            rows = slice(k * tile, (k + 1) * tile)
            turned_ref[which, rows, :width] = (re * c + im * s).astype(jnp.bfloat16)
            turned_ref[which, rows, width:] = (im * c - re * s).astype(jnp.bfloat16)
        spec = jnp.dot(turned_ref[which], ahead_ref[...], preferred_element_type=jnp.float32)
        specs.append((spec[:, :width], spec[:, width:]))
    (m_re, m_im), (g_re, g_im), (f_re, f_im) = specs
    results = (
        (f_re * m_re - f_im * m_im, f_re * m_im + f_im * m_re),
        (f_re * g_re + f_im * g_im, f_re * g_im - f_im * g_re),
        (g_re * m_re + g_im * m_im, g_im * m_re - g_re * m_im),
    )
    for which, (re, im) in enumerate(results):
        both = jnp.concatenate([re.astype(jnp.bfloat16), im.astype(jnp.bfloat16)], axis=1)
        back = jnp.dot(both, back_ref[...], preferred_element_type=jnp.float32)
        values = []
        for k in range(shards):
            rows = slice(k * tile, (k + 1) * tile)
            re, im = back[rows, :width], back[rows, width:]
            c, s = twist_ref[k, 2:3, :], twist_ref[k, 3:4, :]
            values.append((re * c - im * s, re * s + im * c))
        for b, part in enumerate(interpolate(values, math.pi / 2)):
            out_ref[b, which] = part.astype(jnp.bfloat16)


def ungate_kernel(part_ref, value_ref, key_ref, cot_ref, gv_ref, gk_ref, gq_ref, gf_ref):
    conv = part_ref[0, 0].astype(jnp.float32)
    grad = part_ref[0, 1].astype(jnp.float32)
    gv_ref[...] = (grad * key_ref[...].astype(jnp.float32)).astype(jnp.bfloat16)
    gk_ref[...] = (grad * value_ref[...].astype(jnp.float32)).astype(jnp.bfloat16)
    gq_ref[...] = (cot_ref[...].astype(jnp.float32) * conv).astype(jnp.bfloat16)
    gf_ref[...] = part_ref[0, 2].astype(jnp.float32)


def shards(values, keys, queries, grad_out, filters):
    count = lax.axis_size("ctx")
    channels, width = values.shape
    chunk = channels // count
    twist, ahead, back = make_tables(count, width)
    rows = pl.BlockSpec((chunk, width), lambda i: (i, 0))
    packed = pl.BlockSpec((1, 3, chunk, width), lambda i: (i, 0, 0, 0))
    sent = pl.pallas_call(
        gate_kernel,
        grid=(count,),
        in_specs=[rows] * 5,
        out_specs=packed,
        out_shape=jax.ShapeDtypeStruct((count, 3, chunk, width), jnp.bfloat16),
    )(values, keys, queries, grad_out, filters)
    held = lax.all_to_all(sent, "ctx", split_axis=0, concat_axis=0, tiled=True)
    whole = lambda *shape: pl.BlockSpec(shape, lambda i: (0,) * len(shape))
    lanes = pl.BlockSpec((count, 3, TILE, width), lambda i: (0, 0, i, 0))
    made = pl.pallas_call(
        spectral_kernel,
        grid=(chunk // TILE,),
        in_specs=[
            lanes,
            whole(count, 4, width),
            whole(2 * width, 2 * width),
            whole(2 * width, 2 * width),
        ],
        out_specs=lanes,
        out_shape=jax.ShapeDtypeStruct((count, 3, chunk, width), jnp.bfloat16),
        scratch_shapes=[pltpu.VMEM((3, count * TILE, 2 * width), jnp.bfloat16)],
        compiler_params=pltpu.CompilerParams(vmem_limit_bytes=48 * 1024 * 1024),
    )(held, twist, ahead, back)
    returned = lax.all_to_all(made, "ctx", split_axis=0, concat_axis=0, tiled=True)
    half = jax.ShapeDtypeStruct((channels, width), jnp.bfloat16)
    return pl.pallas_call(
        ungate_kernel,
        grid=(count,),
        in_specs=[packed, rows, rows, rows],
        out_specs=[rows] * 4,
        out_shape=[half, half, half, jax.ShapeDtypeStruct((channels, width), jnp.float32)],
    )(returned, values, keys, grad_out)


def solution(mesh):
    token = P(None, ("groups", "ctx"))
    return jax.shard_map(
        shards,
        mesh=mesh,
        in_specs=(token, token, token, token, P(None, "ctx")),
        out_specs=(token, token, token, token),
        check_vma=False,
    )
```

```python
import math

import jax
import jax.numpy as jnp
import numpy as np
from jax import lax
from jax.experimental import pallas as pl
from jax.experimental.pallas import tpu as pltpu
from jax.sharding import PartitionSpec as P

TILE = 16
STEPS = 4


def leaf_angles(count, theta=math.pi / 2):
    if count == 1:
        return [theta]
    half = theta / 2
    return leaf_angles(count // 2, half) + leaf_angles(count // 2, half + math.pi)


def evaluate(points, theta):
    count = len(points)
    if count == 1:
        return points
    half, phi = count // 2, theta / 2
    c, s = math.cos(phi), math.sin(phi)
    first, second = [], []
    for low, high in zip(points[:half], points[half:]):
        if low[1] is None:
            turned_re, turned_im = high[0] * c, high[0] * -s
            first.append((low[0] + turned_re, turned_im))
            second.append((low[0] - turned_re, -turned_im))
        else:
            turned_re = high[0] * c + high[1] * s
            turned_im = high[1] * c - high[0] * s
            first.append((low[0] + turned_re, low[1] + turned_im))
            second.append((low[0] - turned_re, low[1] - turned_im))
    return evaluate(first, phi) + evaluate(second, phi + math.pi)


def interpolate(values, theta, top=True):
    count = len(values)
    if count == 1:
        return values
    half, phi = count // 2, theta / 2
    c, s = math.cos(phi), math.sin(phi)
    first = interpolate(values[:half], phi, False)
    second = interpolate(values[half:], phi + math.pi, False)
    low, high = [], []
    for (a_re, a_im), (b_re, b_im) in zip(first, second):
        gap_re, gap_im = a_re - b_re, a_im - b_im
        if top:
            low.append(a_re + b_re)
            high.append(gap_re * c - gap_im * s)
        else:
            low.append((a_re + b_re, a_im + b_im))
            high.append((gap_re * c - gap_im * s, gap_re * s + gap_im * c))
    return low + high


def make_tables(shards, width):
    angles = np.array(leaf_angles(shards))
    turn = np.outer(angles, np.arange(width)) / width
    scale = 1.0 / (shards * width)
    twist = np.stack(
        [np.cos(turn), np.sin(turn), np.cos(turn) * scale, np.sin(turn) * scale], axis=1
    ).astype(np.float32)
    wave = np.outer(np.arange(width), np.arange(width)) % width * (2 * math.pi / width)
    c, s = np.cos(wave), np.sin(wave)
    ahead = np.block([[c, -s], [s, c]])
    return twist, jnp.asarray(ahead, jnp.bfloat16), jnp.asarray(ahead.T, jnp.bfloat16)


def gate_kernel(value_ref, key_ref, query_ref, cot_ref, filter_ref, out_ref):
    blocks, _, chunk, width = out_ref.shape
    shape = (blocks, chunk, width)
    mixed = value_ref[...].astype(jnp.float32) * key_ref[...].astype(jnp.float32)
    grad = cot_ref[...].astype(jnp.float32) * query_ref[...].astype(jnp.float32)
    out_ref[:, 0] = mixed.astype(jnp.bfloat16).reshape(shape)
    out_ref[:, 1] = grad.astype(jnp.bfloat16).reshape(shape)
    out_ref[:, 2] = filter_ref[...].astype(jnp.bfloat16).reshape(shape)


def spectral_kernel(sig_ref, twist_ref, ahead_ref, back_ref, out_ref, turned_ref):
    shards, _, chunk, width = sig_ref.shape

    @pl.loop(0, chunk // TILE)
    def _(step):
        lanes = pl.ds(pl.multiple_of(step * TILE, TILE), TILE)
        spectral_tile(
            sig_ref.at[:, :, lanes], twist_ref, ahead_ref, back_ref, out_ref.at[:, :, lanes], turned_ref
        )


def spectral_tile(sig_ref, twist_ref, ahead_ref, back_ref, out_ref, turned_ref):
    shards, _, tile, width = sig_ref.shape
    specs = []
    for which in range(3):
        points = [(sig_ref[b, which].astype(jnp.float32), None) for b in range(shards)]
        for k, (re, im) in enumerate(evaluate(points, math.pi / 2)):
            c, s = twist_ref[k, 0:1, :], twist_ref[k, 1:2, :]
            rows = slice(k * tile, (k + 1) * tile)
            turned_ref[which, rows, :width] = (re * c + im * s).astype(jnp.bfloat16)
            turned_ref[which, rows, width:] = (im * c - re * s).astype(jnp.bfloat16)
        spec = jnp.dot(turned_ref[which], ahead_ref[...], preferred_element_type=jnp.float32)
        specs.append((spec[:, :width], spec[:, width:]))
    (m_re, m_im), (g_re, g_im), (f_re, f_im) = specs
    results = (
        (f_re * m_re - f_im * m_im, f_re * m_im + f_im * m_re),
        (f_re * g_re + f_im * g_im, f_re * g_im - f_im * g_re),
        (g_re * m_re + g_im * m_im, g_im * m_re - g_re * m_im),
    )
    for which, (re, im) in enumerate(results):
        both = jnp.concatenate([re.astype(jnp.bfloat16), im.astype(jnp.bfloat16)], axis=1)
        back = jnp.dot(both, back_ref[...], preferred_element_type=jnp.float32)
        values = []
        for k in range(shards):
            rows = slice(k * tile, (k + 1) * tile)
            re, im = back[rows, :width], back[rows, width:]
            c, s = twist_ref[k, 2:3, :], twist_ref[k, 3:4, :]
            values.append((re * c - im * s, re * s + im * c))
        for b, part in enumerate(interpolate(values, math.pi / 2)):
            out_ref[b, which] = part.astype(jnp.bfloat16)


def ungate_kernel(part_ref, value_ref, key_ref, cot_ref, gv_ref, gk_ref, gq_ref, gf_ref):
    _, _, chunk, width = part_ref.shape
    span = gv_ref.shape[0]
    step = pl.program_id(0)
    blocks = pl.ds(step * (span // chunk), span // chunk)
    rows = pl.ds(pl.multiple_of(step * span, span), span)
    conv, grad, filt = (
        part_ref[blocks, which].astype(jnp.float32).reshape(span, width) for which in range(3)
    )
    gv_ref[...] = (grad * key_ref[rows].astype(jnp.float32)).astype(jnp.bfloat16)
    gk_ref[...] = (grad * value_ref[rows].astype(jnp.float32)).astype(jnp.bfloat16)
    gq_ref[...] = (cot_ref[rows].astype(jnp.float32) * conv).astype(jnp.bfloat16)
    gf_ref[...] = filt


def shards(values, keys, queries, grad_out, filters):
    count = lax.axis_size("ctx")
    channels, width = values.shape
    chunk = channels // count
    twist, ahead, back = make_tables(count, width)
    rows = pl.BlockSpec((channels // STEPS, width), lambda i: (i, 0))
    packed = pl.BlockSpec((count // STEPS, 3, chunk, width), lambda i: (i, 0, 0, 0))
    here = pl.BlockSpec(memory_space=pltpu.VMEM)
    limit = pltpu.CompilerParams(vmem_limit_bytes=48 * 1024 * 1024)
    sent = pl.pallas_call(
        gate_kernel,
        grid=(STEPS,),
        in_specs=[rows] * 5,
        out_specs=packed,
        out_shape=jax.ShapeDtypeStruct((count, 3, chunk, width), jnp.bfloat16),
        compiler_params=limit,
    )(values, keys, queries, grad_out, filters)
    held = lax.all_to_all(sent, "ctx", split_axis=0, concat_axis=0, tiled=True)
    made = pl.pallas_call(
        spectral_kernel,
        in_specs=[here] * 4,
        out_specs=here,
        out_shape=jax.ShapeDtypeStruct((count, 3, chunk, width), jnp.bfloat16),
        scratch_shapes=[pltpu.VMEM((3, count * TILE, 2 * width), jnp.bfloat16)],
        compiler_params=limit,
    )(held, twist, ahead, back)
    returned = lax.all_to_all(made, "ctx", split_axis=0, concat_axis=0, tiled=True)
    half = jax.ShapeDtypeStruct((channels, width), jnp.bfloat16)
    return pl.pallas_call(
        ungate_kernel,
        grid=(STEPS,),
        in_specs=[here] * 4,
        out_specs=[rows] * 4,
        out_shape=[half, half, half, jax.ShapeDtypeStruct((channels, width), jnp.float32)],
        compiler_params=limit,
    )(returned, values, keys, grad_out)


def solution(mesh):
    token = P(None, ("groups", "ctx"))
    return jax.shard_map(
        shards,
        mesh=mesh,
        in_specs=(token, token, token, token, P(None, "ctx")),
        out_specs=(token, token, token, token),
        check_vma=False,
    )
```

```python
import math

import jax
import jax.numpy as jnp
import numpy as np
from jax import lax
from jax.experimental import pallas as pl
from jax.experimental.pallas import tpu as pltpu
from jax.sharding import PartitionSpec as P

TILE = 16
STEPS = 4


def leaf_angles(count, theta=math.pi / 2):
    if count == 1:
        return [theta]
    half = theta / 2
    return leaf_angles(count // 2, half) + leaf_angles(count // 2, half + math.pi)


def evaluate(points, theta):
    count = len(points)
    if count == 1:
        return points
    half, phi = count // 2, theta / 2
    c, s = math.cos(phi), math.sin(phi)
    first, second = [], []
    for low, high in zip(points[:half], points[half:]):
        if low[1] is None:
            turned_re, turned_im = high[0] * c, high[0] * -s
            first.append((low[0] + turned_re, turned_im))
            second.append((low[0] - turned_re, -turned_im))
        else:
            turned_re = high[0] * c + high[1] * s
            turned_im = high[1] * c - high[0] * s
            first.append((low[0] + turned_re, low[1] + turned_im))
            second.append((low[0] - turned_re, low[1] - turned_im))
    return evaluate(first, phi) + evaluate(second, phi + math.pi)


def interpolate(values, theta, top=True):
    count = len(values)
    if count == 1:
        return values
    half, phi = count // 2, theta / 2
    c, s = math.cos(phi), math.sin(phi)
    first = interpolate(values[:half], phi, False)
    second = interpolate(values[half:], phi + math.pi, False)
    low, high = [], []
    for (a_re, a_im), (b_re, b_im) in zip(first, second):
        gap_re, gap_im = a_re - b_re, a_im - b_im
        if top:
            low.append(a_re + b_re)
            high.append(gap_re * c - gap_im * s)
        else:
            low.append((a_re + b_re, a_im + b_im))
            high.append((gap_re * c - gap_im * s, gap_re * s + gap_im * c))
    return low + high


def make_tables(shards, width):
    angles = np.array(leaf_angles(shards))
    turn = np.outer(angles, np.arange(width)) / width
    scale = 1.0 / (shards * width)
    twist = np.stack(
        [np.cos(turn), np.sin(turn), np.cos(turn) * scale, np.sin(turn) * scale], axis=1
    ).astype(np.float32)
    wave = np.outer(np.arange(width), np.arange(width)) % width * (2 * math.pi / width)
    c, s = np.cos(wave), np.sin(wave)
    ahead = np.block([[c, -s], [s, c]])
    return twist, jnp.asarray(ahead, jnp.bfloat16), jnp.asarray(ahead.T, jnp.bfloat16)


def gate_kernel(value_ref, key_ref, query_ref, cot_ref, out_ref):
    blocks, _, chunk, width = out_ref.shape
    shape = (blocks, chunk, width)
    mixed = value_ref[...].astype(jnp.float32) * key_ref[...].astype(jnp.float32)
    grad = cot_ref[...].astype(jnp.float32) * query_ref[...].astype(jnp.float32)
    out_ref[:, 0] = mixed.astype(jnp.bfloat16).reshape(shape)
    out_ref[:, 1] = grad.astype(jnp.bfloat16).reshape(shape)


def transform(points, twist_ref, ahead_ref, turned_ref):
    tile, width = points[0].shape
    points = [(point.astype(jnp.float32), None) for point in points]
    for k, (re, im) in enumerate(evaluate(points, math.pi / 2)):
        c, s = twist_ref[k, 0:1, :], twist_ref[k, 1:2, :]
        rows = slice(k * tile, (k + 1) * tile)
        turned_ref[rows, :width] = (re * c + im * s).astype(jnp.bfloat16)
        turned_ref[rows, width:] = (im * c - re * s).astype(jnp.bfloat16)
    return jnp.dot(turned_ref[...], ahead_ref[...], preferred_element_type=jnp.float32)


def inverse(re, im, twist_ref, back_ref):
    count, _, width = twist_ref.shape
    tile = re.shape[0] // count
    both = jnp.concatenate([re.astype(jnp.bfloat16), im.astype(jnp.bfloat16)], axis=1)
    back = jnp.dot(both, back_ref[...], preferred_element_type=jnp.float32)
    values = []
    for k in range(count):
        rows = slice(k * tile, (k + 1) * tile)
        re, im = back[rows, :width], back[rows, width:]
        c, s = twist_ref[k, 2:3, :], twist_ref[k, 3:4, :]
        values.append((re * c - im * s, re * s + im * c))
    return interpolate(values, math.pi / 2)


def filter_kernel(mine_ref, other_ref, twist_ref, ahead_ref, spec_ref, turned_ref):
    near, far, rows, _ = mine_ref.shape
    me, side = lax.axis_index("ctx"), lax.axis_index("groups")

    def piece(share_ref, b, lanes):
        return share_ref[(me % near) ^ (b % near), (me // near) ^ (b // near), lanes]

    def points(first, lanes):
        return [
            jnp.where(side == first, piece(mine_ref, b, lanes), piece(other_ref, b, lanes))
            for b in range(near * far)
        ]

    if rows < TILE:
        parts = zip(*[points(half, slice(None)) for half in range(2)])
        joined = [jnp.concatenate([p.astype(jnp.float32) for p in pair]) for pair in parts]
        spec_ref[0] = transform(joined, twist_ref, ahead_ref, turned_ref)
    else:
        for half in range(2):

            @pl.loop(0, rows // TILE)
            def _(step):
                lanes = pl.ds(pl.multiple_of(step * TILE, TILE), TILE)
                spec_ref[half * (rows // TILE) + step] = transform(
                    points(half, lanes), twist_ref, ahead_ref, turned_ref
                )


def spectral_kernel(sig_ref, spec_ref, twist_ref, ahead_ref, back_ref, out_ref, turned_ref):
    count, _, chunk, width = sig_ref.shape

    @pl.loop(0, chunk // TILE)
    def _(step):
        lanes = pl.ds(pl.multiple_of(step * TILE, TILE), TILE)
        specs = []
        for which in range(2):
            points = [sig_ref[b, which, lanes] for b in range(count)]
            spec = transform(points, twist_ref, ahead_ref, turned_ref.at[which])
            specs.append((spec[:, :width], spec[:, width:]))
        (m_re, m_im), (g_re, g_im) = specs
        f_re, f_im = spec_ref[step, :, :width], spec_ref[step, :, width:]
        results = (
            (f_re * m_re - f_im * m_im, f_re * m_im + f_im * m_re),
            (f_re * g_re + f_im * g_im, f_re * g_im - f_im * g_re),
            (g_re * m_re + g_im * m_im, g_im * m_re - g_re * m_im),
        )
        for which, (re, im) in enumerate(results):
            for b, part in enumerate(inverse(re, im, twist_ref, back_ref)):
                out_ref[b, which, lanes] = part.astype(jnp.bfloat16)


def ungate_kernel(part_ref, value_ref, key_ref, cot_ref, gv_ref, gk_ref, gq_ref, gf_ref):
    _, _, chunk, width = part_ref.shape
    span = gv_ref.shape[0]
    step = pl.program_id(0)
    blocks = pl.ds(step * (span // chunk), span // chunk)
    rows = pl.ds(pl.multiple_of(step * span, span), span)
    conv, grad, filt = (
        part_ref[blocks, which].astype(jnp.float32).reshape(span, width) for which in range(3)
    )
    gv_ref[...] = (grad * key_ref[rows].astype(jnp.float32)).astype(jnp.bfloat16)
    gk_ref[...] = (grad * value_ref[rows].astype(jnp.float32)).astype(jnp.bfloat16)
    gq_ref[...] = (cot_ref[rows].astype(jnp.float32) * conv).astype(jnp.bfloat16)
    gf_ref[...] = filt


def exchange(parts):
    return lax.all_to_all(parts, "ctx", split_axis=0, concat_axis=0, tiled=True)


def swap(block, axis, gap):
    size = lax.axis_size(axis)
    return lax.ppermute(block, axis, [(i, i ^ gap) for i in range(size)])


def pick(blocks, where):
    return lax.dynamic_index_in_dim(blocks, where, 0, keepdims=False)


def far_filters(filters, far):
    count, me, side = lax.axis_size("ctx"), lax.axis_index("ctx"), lax.axis_index("groups")
    near = count // far
    channels, width = filters.shape
    share = filters.reshape(far, near, 2, channels // count // 2, width)
    share = lax.dynamic_index_in_dim(share, side, 2, keepdims=False)
    blocks = [pick(share, (me // near) ^ k).astype(jnp.bfloat16) for k in range(far)]
    return blocks[:1] + [swap(blocks[k], "ctx", k * near) for k in range(1, far)]


def near_filters(blocks):
    me, near = lax.axis_index("ctx"), blocks[0].shape[0]
    parts = [jnp.stack([pick(b, (me % near) ^ j) for b in blocks]) for j in range(near)]
    mine = jnp.stack(parts[:1] + [swap(parts[j], "ctx", j) for j in range(1, near)])
    return mine, swap(mine, "groups", 1)


def shards(values, keys, queries, grad_out, filters):
    count = lax.axis_size("ctx")
    channels, width = values.shape
    chunk = channels // count
    twist, ahead, back = make_tables(count, width)
    rows = pl.BlockSpec((channels // STEPS, width), lambda i: (i, 0))
    here = pl.BlockSpec(memory_space=pltpu.VMEM)
    limit = pltpu.CompilerParams(vmem_limit_bytes=48 * 1024 * 1024)
    far = 1 << ((count.bit_length() - 1) // 2)
    blocks = far_filters(filters, far)
    sent = pl.pallas_call(
        gate_kernel,
        in_specs=[here] * 4,
        out_specs=here,
        out_shape=jax.ShapeDtypeStruct((count, 2, chunk, width), jnp.bfloat16),
        compiler_params=limit,
    )(values, keys, queries, grad_out)
    blocks, sent = lax.optimization_barrier((blocks, sent))
    held = exchange(sent)
    mine, other = near_filters(blocks)
    tall = count * TILE
    spec = pl.pallas_call(
        filter_kernel,
        in_specs=[here] * 4,
        out_specs=here,
        out_shape=jax.ShapeDtypeStruct((chunk // TILE, tall, 2 * width), jnp.float32),
        scratch_shapes=[pltpu.VMEM((tall, 2 * width), jnp.bfloat16)],
        compiler_params=limit,
        cost_estimate=pl.CostEstimate(
            flops=8 * count * chunk * width * width, bytes_accessed=2**20, transcendentals=0
        ),
    )(mine, other, twist, ahead)
    made = pl.pallas_call(
        spectral_kernel,
        in_specs=[here] * 5,
        out_specs=here,
        out_shape=jax.ShapeDtypeStruct((count, 3, chunk, width), jnp.bfloat16),
        scratch_shapes=[pltpu.VMEM((2, tall, 2 * width), jnp.bfloat16)],
        compiler_params=limit,
    )(held, spec, twist, ahead, back)
    returned = exchange(made)
    half = jax.ShapeDtypeStruct((channels, width), jnp.bfloat16)
    return pl.pallas_call(
        ungate_kernel,
        grid=(STEPS,),
        in_specs=[here] * 4,
        out_specs=[rows] * 4,
        out_shape=[half, half, half, jax.ShapeDtypeStruct((channels, width), jnp.float32)],
        compiler_params=limit,
    )(returned, values, keys, grad_out)


def solution(mesh):
    token = P(None, ("groups", "ctx"))
    return jax.shard_map(
        shards,
        mesh=mesh,
        in_specs=(token, token, token, token, P(None, "ctx")),
        out_specs=(token, token, token, token),
        check_vma=False,
    )
```

```python
import math

import jax
import jax.numpy as jnp
import numpy as np
from jax import lax
from jax.experimental import pallas as pl
from jax.experimental.pallas import tpu as pltpu
from jax.sharding import PartitionSpec as P

TILE = 32
STEPS = 4


def evaluate(points, theta):
    count = len(points)
    if count == 1:
        return [(theta, *points[0])]
    half, phi = count // 2, theta / 2
    c, s = math.cos(phi), math.sin(phi)
    first, second = [], []
    for (low_re, low_im), (high_re, high_im) in zip(points[:half], points[half:]):
        if theta == math.pi / 2:
            turned_re, turned_im = (high_re + high_im) * c, (high_im - high_re) * c
        else:
            turned_re, turned_im = high_re * c + high_im * s, high_im * c - high_re * s
        first.append((low_re + turned_re, low_im + turned_im))
        second.append((low_re - turned_re, low_im - turned_im))
    return evaluate(first, phi) + evaluate(second, phi + math.pi)


def interpolate(values, theta):
    count = len(values)
    if count == 1:
        return values
    half, phi = count // 2, theta / 2
    c, s = math.cos(phi), math.sin(phi)
    first = interpolate(values[:half], phi)
    second = interpolate(values[half:], phi + math.pi)
    low, high = [], []
    for (a_re, a_im), (b_re, b_im) in zip(first, second):
        gap_re, gap_im = a_re - b_re, a_im - b_im
        low.append((a_re + b_re, a_im + b_im))
        if theta == math.pi / 2:
            high.append(((gap_re - gap_im) * c, (gap_re + gap_im) * c))
        else:
            high.append((gap_re * c - gap_im * s, gap_re * s + gap_im * c))
    return low + high


def odd_values(points):
    half = len(points) // 2
    return evaluate([(low, -high) for low, high in zip(points[:half], points[half:])], math.pi / 2)


def odd_points(values):
    turned = interpolate(values, math.pi / 2)
    return [re for re, _ in turned] + [-im for _, im in turned]


def even_values(points):
    if len(points) == 2:
        return [points[0] + points[1], points[0] - points[1]]
    half = len(points) // 2
    pairs = list(zip(points[:half], points[half:]))
    return even_values([a + b for a, b in pairs]) + odd_values([a - b for a, b in pairs])


def even_points(values, count):
    if count == 2:
        return [values[0] + values[1], values[0] - values[1]]
    split = count // 4 + 1
    even, odd = even_points(values[:split], count // 2), odd_points(values[split:])
    return [a + b for a, b in zip(even, odd)] + [a - b for a, b in zip(even, odd)]


def short_values(points):
    return even_values(points) + odd_values(points)


def short_points(values, count):
    split = count // 2 + 1
    even, odd = even_points(values[:split], count), odd_points(values[split:])
    return [a + b for a, b in zip(even, odd)]


def short_angles(count):
    zero = [(0.0, 0.0)] * count
    odd = lambda n: [angle for angle, *_ in evaluate(zero[: n // 2], math.pi / 2)]
    sizes, even = [count], count
    while even > 2:
        even //= 2
        sizes.append(even)
    return [0.0, math.pi] + sum((odd(n) for n in reversed(sizes)), [])


def make_tables(count, width):
    angles = np.array(short_angles(count))
    turn = np.outer(angles, np.arange(width)) / width
    scale = np.where(np.arange(len(angles)) < 2, 1.0, 2.0)[:, None] / (2 * count * width)
    twist = np.stack(
        [np.cos(turn), np.sin(turn), np.cos(turn) * scale, np.sin(turn) * scale], axis=1
    ).astype(np.float32)
    wave = np.outer(np.arange(width), np.arange(width)) % width * (2 * math.pi / width)
    c, s = np.cos(wave), np.sin(wave)
    ahead = np.block([[c, -s], [s, c]])
    return twist, jnp.asarray(np.stack([ahead, ahead.T]), jnp.bfloat16)


def gate_kernel(value_hbm, key_hbm, cot_hbm, query_hbm, out_hbm, *scratch):
    blocks, _, chunk, width = out_hbm.shape
    sources = (value_hbm, key_hbm, cot_hbm, query_hbm)
    *held, made, loads, stores = scratch
    span, some = blocks * chunk // STEPS, blocks // STEPS
    copies = []
    for step in range(STEPS):
        rows = pl.ds(step * span, span)
        copies.append(
            [
                pltpu.make_async_copy(source.at[rows], to.at[rows], loads.at[i, step])
                for i, (source, to) in enumerate(zip(sources, held))
            ]
        )
        for copy in copies[-1]:
            copy.start()
    sends = []
    for step in range(STEPS):
        for copy in copies[step]:
            copy.wait()
        rows, part = pl.ds(step * span, span), pl.ds(step * some, some)
        for which in range(2):
            left, right = held[2 * which][rows], held[2 * which + 1][rows]
            both = left.astype(jnp.float32) * right.astype(jnp.float32)
            made[part, which] = both.astype(jnp.bfloat16).reshape(some, chunk, width)
        sends.append(pltpu.make_async_copy(made.at[part], out_hbm.at[part], stores.at[step]))
        sends[-1].start()
    for send in sends:
        send.wait()


def transform(points, twist_ref, wave_ref, turned_ref):
    tile, width = points[0].shape
    points = [point.astype(jnp.float32) for point in points]
    for top in range(0, tile, 16):
        halves = []
        for start in (top, top + 8):
            done = []
            for k, value in enumerate(short_values([p[start : start + 8] for p in points])):
                c, s = twist_ref[k, 0:1, :], twist_ref[k, 1:2, :]
                if k == 0:
                    re, im = value, jnp.zeros_like(value)
                elif k == 1:
                    re, im = value * c, value * -s
                else:
                    _, re, im = value
                    re, im = re * c + im * s, im * c - re * s
                done.append((re, im))
            halves.append(done)
        for k, ((a_re, a_im), (b_re, b_im)) in enumerate(zip(*halves)):
            rows = slice(k * tile + top, k * tile + top + 16)
            turned_ref[rows, :width] = jnp.concatenate([a_re, b_re]).astype(jnp.bfloat16)
            turned_ref[rows, width:] = jnp.concatenate([a_im, b_im]).astype(jnp.bfloat16)
    return jnp.dot(turned_ref[...], wave_ref[0], preferred_element_type=jnp.float32)


def inverse(re, im, twist_ref, wave_ref):
    count, _, width = twist_ref.shape
    tile = re.shape[0] // count
    both = jnp.concatenate([re.astype(jnp.bfloat16), im.astype(jnp.bfloat16)], axis=1)
    back = jnp.dot(both, wave_ref[1], preferred_element_type=jnp.float32)
    parts = []
    for start in range(0, tile, 8):
        values = []
        for k in range(count):
            rows = slice(k * tile + start, k * tile + start + 8)
            re, im = back[rows, :width], back[rows, width:]
            c, s = twist_ref[k, 2:3, :], twist_ref[k, 3:4, :]
            if k == 0:
                values.append(re * c)
            elif k == 1:
                values.append(re * c - im * s)
            else:
                values.append((re * c - im * s, re * s + im * c))
        parts.append(short_points(values, count - 1))
    return [jnp.concatenate(part) for part in zip(*parts)]


def filter_kernel(mine_ref, other_ref, twist_ref, wave_ref, spec_ref, turned_ref):
    near, far, rows, _ = mine_ref.shape
    tile = spec_ref.shape[1] // twist_ref.shape[0]
    me, side = lax.axis_index("ctx"), lax.axis_index("groups")

    def piece(share_ref, b, lanes):
        return share_ref[(me % near) ^ (b % near), (me // near) ^ (b // near), lanes]

    def points(first, lanes):
        return [
            jnp.where(side == first, piece(mine_ref, b, lanes), piece(other_ref, b, lanes))
            for b in range(near * far)
        ]

    if rows < tile:
        parts = zip(*[points(half, slice(None)) for half in range(2)])
        joined = [jnp.concatenate([p.astype(jnp.float32) for p in pair]) for pair in parts]
        spec = transform(joined, twist_ref, wave_ref, turned_ref)
        spec_ref[0] = spec.astype(jnp.bfloat16)
    else:
        for half in range(2):

            @pl.loop(0, rows // tile)
            def _(step):
                lanes = pl.ds(pl.multiple_of(step * tile, tile), tile)
                spec = transform(points(half, lanes), twist_ref, wave_ref, turned_ref)
                spec_ref[half * (rows // tile) + step] = spec.astype(jnp.bfloat16)


def spectral_kernel(sig_ref, spec_ref, twist_ref, wave_ref, out_ref, turned_ref):
    count, _, chunk, width = sig_ref.shape
    tile = spec_ref.shape[1] // twist_ref.shape[0]

    @pl.loop(0, chunk // tile)
    def _(step):
        lanes = pl.ds(pl.multiple_of(step * tile, tile), tile)
        specs = []
        for which in range(2):
            points = [sig_ref[b, which, lanes] for b in range(count)]
            spec = transform(points, twist_ref, wave_ref, turned_ref.at[which])
            specs.append((spec[:, :width], spec[:, width:]))
        (m_re, m_im), (g_re, g_im) = specs
        spec = spec_ref[step].astype(jnp.float32)
        f_re, f_im = spec[:, :width], spec[:, width:]
        results = (
            (f_re * m_re - f_im * m_im, f_re * m_im + f_im * m_re),
            (f_re * g_re + f_im * g_im, f_re * g_im - f_im * g_re),
            (g_re * m_re + g_im * m_im, g_im * m_re - g_re * m_im),
        )
        for which, (re, im) in enumerate(results):
            for b, part in enumerate(inverse(re, im, twist_ref, wave_ref)):
                out_ref[b, which, lanes] = part.astype(jnp.bfloat16)


def ungate_kernel(part_ref, value_ref, key_ref, cot_ref, gv_hbm, gk_hbm, gq_hbm, gf_hbm, *scratch):
    blocks, _, chunk, width = part_ref.shape
    outs = (gv_hbm, gk_hbm, gq_hbm, gf_hbm)
    *made, sems = scratch
    span, some = blocks * chunk // STEPS, blocks // STEPS
    sends = []
    for step in range(STEPS):
        rows, part = pl.ds(step * span, span), pl.ds(step * some, some)
        conv, grad, filt = (
            part_ref[part, which].astype(jnp.float32).reshape(span, width) for which in range(3)
        )
        made[0][rows] = (grad * key_ref[rows].astype(jnp.float32)).astype(jnp.bfloat16)
        made[1][rows] = (grad * value_ref[rows].astype(jnp.float32)).astype(jnp.bfloat16)
        made[2][rows] = (cot_ref[rows].astype(jnp.float32) * conv).astype(jnp.bfloat16)
        made[3][rows] = filt
        for i, (source, to) in enumerate(zip(made, outs)):
            sends.append(pltpu.make_async_copy(source.at[rows], to.at[rows], sems.at[i, step]))
            sends[-1].start()
    for send in sends:
        send.wait()


def exchange(parts):
    return lax.all_to_all(parts, "ctx", split_axis=0, concat_axis=0, tiled=True)


def swap(block, axis, gap):
    size = lax.axis_size(axis)
    return lax.ppermute(block, axis, [(i, i ^ gap) for i in range(size)])


def pick(blocks, where):
    return lax.dynamic_index_in_dim(blocks, where, 0, keepdims=False)


def far_filters(filters, far):
    count, me, side = lax.axis_size("ctx"), lax.axis_index("ctx"), lax.axis_index("groups")
    near = count // far
    channels, width = filters.shape
    share = filters.reshape(far, near, 2, channels // count // 2, width)
    share = lax.dynamic_index_in_dim(share, side, 2, keepdims=False)
    blocks = [pick(share, (me // near) ^ k).astype(jnp.bfloat16) for k in range(far)]
    return blocks[:1] + [swap(blocks[k], "ctx", k * near) for k in range(1, far)]


def near_filters(blocks):
    me, near = lax.axis_index("ctx"), blocks[0].shape[0]
    parts = [jnp.stack([pick(b, (me % near) ^ j) for b in blocks]) for j in range(near)]
    mine = jnp.stack(parts[:1] + [swap(parts[j], "ctx", j) for j in range(1, near)])
    return mine, swap(mine, "groups", 1)


def shards(values, keys, queries, grad_out, filters):
    count = lax.axis_size("ctx")
    channels, width = values.shape
    chunk = channels // count
    twist, wave = make_tables(count, width)
    here = pl.BlockSpec(memory_space=pltpu.VMEM)
    limit = pltpu.CompilerParams(vmem_limit_bytes=24 * 1024 * 1024)
    far = 1 << ((count.bit_length() - 1) // 2)
    blocks = far_filters(filters, far)
    hbm = pl.BlockSpec(memory_space=pl.ANY)
    sent = pl.pallas_call(
        gate_kernel,
        in_specs=[hbm] * 4,
        out_specs=hbm,
        out_shape=jax.ShapeDtypeStruct((count, 2, chunk, width), jnp.bfloat16),
        scratch_shapes=[pltpu.VMEM((channels, width), jnp.bfloat16)] * 4
        + [
            pltpu.VMEM((count, 2, chunk, width), jnp.bfloat16),
            pltpu.SemaphoreType.DMA((4, STEPS)),
            pltpu.SemaphoreType.DMA((STEPS,)),
        ],
    )(values, keys, grad_out, queries)
    blocks, sent = lax.optimization_barrier((blocks, sent))
    held = exchange(sent)
    mine, other = near_filters(blocks)
    tile = min(TILE, chunk)
    tall = (count + 1) * tile
    spec = pl.pallas_call(
        filter_kernel,
        in_specs=[here] * 4,
        out_specs=here,
        out_shape=jax.ShapeDtypeStruct((chunk // tile, tall, 2 * width), jnp.bfloat16),
        scratch_shapes=[pltpu.VMEM((tall, 2 * width), jnp.bfloat16)],
        compiler_params=limit,
        cost_estimate=pl.CostEstimate(
            flops=8 * count * chunk * width * width, bytes_accessed=2**20, transcendentals=0
        ),
    )(mine, other, twist, wave)
    made = pl.pallas_call(
        spectral_kernel,
        in_specs=[here] * 4,
        out_specs=here,
        out_shape=jax.ShapeDtypeStruct((count, 3, chunk, width), jnp.bfloat16),
        scratch_shapes=[pltpu.VMEM((2, tall, 2 * width), jnp.bfloat16)],
        compiler_params=limit,
    )(held, spec, twist, wave)
    returned = exchange(made)
    half = jax.ShapeDtypeStruct((channels, width), jnp.bfloat16)
    wide = jax.ShapeDtypeStruct((channels, width), jnp.float32)
    return pl.pallas_call(
        ungate_kernel,
        in_specs=[here] * 4,
        out_specs=[hbm] * 4,
        out_shape=[half, half, half, wide],
        scratch_shapes=[pltpu.VMEM((channels, width), jnp.bfloat16)] * 3
        + [pltpu.VMEM((channels, width), jnp.float32), pltpu.SemaphoreType.DMA((4, STEPS))],
        compiler_params=limit,
    )(returned, values, keys, grad_out)


def solution(mesh):
    token = P(None, ("groups", "ctx"))
    return jax.shard_map(
        shards,
        mesh=mesh,
        in_specs=(token, token, token, token, P(None, "ctx")),
        out_specs=(token, token, token, token),
        check_vma=False,
    )
```

```python
import functools
import math

import jax
import jax.numpy as jnp
import numpy as np
from jax import lax
from jax.experimental import pallas as pl
from jax.experimental.pallas import tpu as pltpu
from jax.sharding import PartitionSpec as P

TILE = 32
STEPS = 4
WINDOW = 6


def evaluate(points, theta):
    count = len(points)
    if count == 1:
        return [(theta, *points[0])]
    half, phi = count // 2, theta / 2
    c, s = math.cos(phi), math.sin(phi)
    first, second = [], []
    for (low_re, low_im), (high_re, high_im) in zip(points[:half], points[half:]):
        if theta == math.pi / 2:
            turned_re, turned_im = (high_re + high_im) * c, (high_im - high_re) * c
        else:
            turned_re, turned_im = high_re * c + high_im * s, high_im * c - high_re * s
        first.append((low_re + turned_re, low_im + turned_im))
        second.append((low_re - turned_re, low_im - turned_im))
    return evaluate(first, phi) + evaluate(second, phi + math.pi)


def interpolate(values, theta):
    count = len(values)
    if count == 1:
        return values
    half, phi = count // 2, theta / 2
    c, s = math.cos(phi), math.sin(phi)
    first = interpolate(values[:half], phi)
    second = interpolate(values[half:], phi + math.pi)
    low, high = [], []
    for (a_re, a_im), (b_re, b_im) in zip(first, second):
        gap_re, gap_im = a_re - b_re, a_im - b_im
        low.append((a_re + b_re, a_im + b_im))
        if theta == math.pi / 2:
            high.append(((gap_re - gap_im) * c, (gap_re + gap_im) * c))
        else:
            high.append((gap_re * c - gap_im * s, gap_re * s + gap_im * c))
    return low + high


def odd_values(points):
    half = len(points) // 2
    return evaluate([(low, -high) for low, high in zip(points[:half], points[half:])], math.pi / 2)


def odd_points(values):
    turned = interpolate(values, math.pi / 2)
    return [re for re, _ in turned] + [-im for _, im in turned]


def even_values(points):
    if len(points) == 2:
        return [points[0] + points[1], points[0] - points[1]]
    half = len(points) // 2
    pairs = list(zip(points[:half], points[half:]))
    return even_values([a + b for a, b in pairs]) + odd_values([a - b for a, b in pairs])


def even_points(values, count):
    if count == 2:
        return [values[0] + values[1], values[0] - values[1]]
    split = count // 4 + 1
    even, odd = even_points(values[:split], count // 2), odd_points(values[split:])
    return [a + b for a, b in zip(even, odd)] + [a - b for a, b in zip(even, odd)]


def short_values(points):
    return even_values(points) + odd_values(points)


def short_points(values, count):
    split = count // 2 + 1
    even, odd = even_points(values[:split], count), odd_points(values[split:])
    return [a + b for a, b in zip(even, odd)]


def short_angles(count):
    zero = [(0.0, 0.0)] * count
    odd = lambda n: [angle for angle, *_ in evaluate(zero[: n // 2], math.pi / 2)]
    sizes, even = [count], count
    while even > 2:
        even //= 2
        sizes.append(even)
    return [0.0, math.pi] + sum((odd(n) for n in reversed(sizes)), [])


def make_tables(count, width):
    angles = np.array(short_angles(count))
    turn = np.outer(angles, np.arange(width)) / width
    scale = np.where(np.arange(len(angles)) < 2, 1.0, 2.0)[:, None] / (2 * count * width)
    twist = np.stack(
        [np.cos(turn), np.sin(turn), np.cos(turn) * scale, np.sin(turn) * scale], axis=1
    ).astype(np.float32)
    wave = np.outer(np.arange(width), np.arange(width)) % width * (2 * math.pi / width)
    c, s = np.cos(wave), np.sin(wave)
    ahead = np.block([[c, -s], [s, c]])
    return twist, jnp.asarray(np.stack([ahead, ahead.T]), jnp.bfloat16)


def rows_of(block, chunk):
    return pl.ds(pl.multiple_of(block * chunk, chunk), chunk)


def gate_kernel(value_hbm, key_hbm, cot_hbm, query_hbm, out_hbm, *scratch):
    blocks, _, chunk, width = out_hbm.shape
    sources = (value_hbm, key_hbm, cot_hbm, query_hbm)
    *held, made, loads, stores = scratch
    span, some = blocks * chunk // STEPS, blocks // STEPS
    copies = []
    for step in range(STEPS):
        rows = pl.ds(step * span, span)
        copies.append(
            [
                pltpu.make_async_copy(source.at[rows], to.at[rows], loads.at[i, step])
                for i, (source, to) in enumerate(zip(sources, held))
            ]
        )
        for copy in copies[-1]:
            copy.start()
    sends = []
    for step in range(STEPS):
        for copy in copies[step]:
            copy.wait()
        rows, part = pl.ds(step * span, span), pl.ds(step * some, some)
        for which in range(2):
            left, right = held[2 * which][rows], held[2 * which + 1][rows]
            both = left.astype(jnp.float32) * right.astype(jnp.float32)
            made[part, which] = both.astype(jnp.bfloat16).reshape(some, chunk, width)
        sends.append(pltpu.make_async_copy(made.at[part], out_hbm.at[part], stores.at[step]))
        sends[-1].start()
    for send in sends:
        send.wait()


def transform(points, twist_ref, wave_ref, turned_ref):
    tile, width = points[0].shape
    points = [point.astype(jnp.float32) for point in points]
    for top in range(0, tile, 16):
        halves = []
        for start in (top, top + 8):
            done = []
            for k, value in enumerate(short_values([p[start : start + 8] for p in points])):
                c, s = twist_ref[k, 0:1, :], twist_ref[k, 1:2, :]
                if k == 0:
                    re, im = value, jnp.zeros_like(value)
                elif k == 1:
                    re, im = value * c, value * -s
                else:
                    _, re, im = value
                    re, im = re * c + im * s, im * c - re * s
                done.append((re, im))
            halves.append(done)
        for k, ((a_re, a_im), (b_re, b_im)) in enumerate(zip(*halves)):
            rows = slice(k * tile + top, k * tile + top + 16)
            turned_ref[rows, :width] = jnp.concatenate([a_re, b_re]).astype(jnp.bfloat16)
            turned_ref[rows, width:] = jnp.concatenate([a_im, b_im]).astype(jnp.bfloat16)
    return jnp.dot(turned_ref[...], wave_ref[0], preferred_element_type=jnp.float32)


def inverse(re, im, twist_ref, wave_ref):
    count, _, width = twist_ref.shape
    tile = re.shape[0] // count
    both = jnp.concatenate([re.astype(jnp.bfloat16), im.astype(jnp.bfloat16)], axis=1)
    back = jnp.dot(both, wave_ref[1], preferred_element_type=jnp.float32)
    parts = []
    for start in range(0, tile, 8):
        values = []
        for k in range(count):
            rows = slice(k * tile + start, k * tile + start + 8)
            re, im = back[rows, :width], back[rows, width:]
            c, s = twist_ref[k, 2:3, :], twist_ref[k, 3:4, :]
            if k == 0:
                values.append(re * c)
            elif k == 1:
                values.append(re * c - im * s)
            else:
                values.append((re * c - im * s, re * s + im * c))
        parts.append(short_points(values, count - 1))
    return [jnp.concatenate(part) for part in zip(*parts)]


def filter_kernel(mine_ref, other_ref, twist_ref, wave_ref, spec_ref, turned_ref):
    near, far, rows, _ = mine_ref.shape
    tile = spec_ref.shape[1] // twist_ref.shape[0]
    me, side = lax.axis_index("ctx"), lax.axis_index("groups")

    def piece(share_ref, b, lanes):
        return share_ref[(me % near) ^ (b % near), (me // near) ^ (b // near), lanes]

    def points(first, lanes):
        return [
            jnp.where(side == first, piece(mine_ref, b, lanes), piece(other_ref, b, lanes))
            for b in range(near * far)
        ]

    if rows < tile:
        parts = zip(*[points(half, slice(None)) for half in range(2)])
        joined = [jnp.concatenate([p.astype(jnp.float32) for p in pair]) for pair in parts]
        spec = transform(joined, twist_ref, wave_ref, turned_ref)
        spec_ref[0] = spec.astype(jnp.bfloat16)
    else:
        for half in range(2):

            @pl.loop(0, rows // tile)
            def _(step):
                lanes = pl.ds(pl.multiple_of(step * tile, tile), tile)
                spec = transform(points(half, lanes), twist_ref, wave_ref, turned_ref)
                spec_ref[half * (rows // tile) + step] = spec.astype(jnp.bfloat16)


def spectral_kernel(sig_ref, spec_ref, twist_ref, wave_ref, *refs):
    *out_refs, made_ref, turned_ref = refs
    count, _, chunk, width = sig_ref.shape
    tile = spec_ref.shape[1] // twist_ref.shape[0]
    me = lax.axis_index("ctx")

    @pl.loop(0, chunk // tile)
    def _(step):
        lanes = rows_of(step, tile)
        specs = []
        for which in range(2):
            points = [sig_ref[b, which, lanes] for b in range(count)]
            spec = transform(points, twist_ref, wave_ref, turned_ref.at[which])
            specs.append((spec[:, :width], spec[:, width:]))
        (m_re, m_im), (g_re, g_im) = specs
        spec = spec_ref[step].astype(jnp.float32)
        f_re, f_im = spec[:, :width], spec[:, width:]
        results = (
            (f_re * m_re - f_im * m_im, f_re * m_im + f_im * m_re),
            (f_re * g_re + f_im * g_im, f_re * g_im - f_im * g_re),
            (g_re * m_re + g_im * m_im, g_im * m_re - g_re * m_im),
        )
        for which, (re, im) in enumerate(results):
            for b, part in enumerate(inverse(re, im, twist_ref, wave_ref)):
                made_ref[b, which, lanes] = part.astype(jnp.bfloat16)

    for k in range(count):
        out_refs[k][...] = made_ref[me ^ k]


def ungate_kernel(which_blocks, *refs):
    *made, sems = refs[-5:]
    outs = refs[-9:-5]
    value_ref, key_ref, cot_ref = refs[:3]
    me = lax.axis_index("ctx")
    sends = []
    for i, k in enumerate(which_blocks):
        part_ref = refs[3 + i]
        rows = rows_of(me ^ k, part_ref.shape[1])
        conv, grad, filt = (part_ref[which].astype(jnp.float32) for which in range(3))
        made[0][rows] = (grad * key_ref[rows].astype(jnp.float32)).astype(jnp.bfloat16)
        made[1][rows] = (grad * value_ref[rows].astype(jnp.float32)).astype(jnp.bfloat16)
        made[2][rows] = (cot_ref[rows].astype(jnp.float32) * conv).astype(jnp.bfloat16)
        made[3][rows] = filt
        for j, (source, to) in enumerate(zip(made, outs)):
            sends.append(pltpu.make_async_copy(source.at[rows], to.at[rows], sems.at[j, i]))
            sends[-1].start()
    for send in sends:
        send.wait()


def partners(count):
    near, size = [], count // 4
    while size:
        near += range(size, 2 * size)
        size //= 2
    far = list(range(count // 2, count))
    order = []
    for i, k in enumerate(far):
        order += [k] + near[i : i + 1]
    return order


def spread(blocks):
    count = len(blocks)
    got = list(blocks)
    order = partners(count)
    for i, k in enumerate(order):
        block = blocks[k]
        if i >= WINDOW:
            before = order[i - WINDOW]
            block, got[before] = lax.optimization_barrier((block, got[before]))
        got[k] = lax.ppermute(block, "ctx", [(j, j ^ k) for j in range(count)])
    return got


def exchange(parts):
    return lax.all_to_all(parts, "ctx", split_axis=0, concat_axis=0, tiled=True)


def swap(block, axis, gap):
    size = lax.axis_size(axis)
    return lax.ppermute(block, axis, [(i, i ^ gap) for i in range(size)])


def pick(blocks, where):
    return lax.dynamic_index_in_dim(blocks, where, 0, keepdims=False)


def far_filters(filters, far):
    count, me, side = lax.axis_size("ctx"), lax.axis_index("ctx"), lax.axis_index("groups")
    near = count // far
    channels, width = filters.shape
    share = filters.reshape(far, near, 2, channels // count // 2, width)
    share = lax.dynamic_index_in_dim(share, side, 2, keepdims=False)
    blocks = [pick(share, (me // near) ^ k).astype(jnp.bfloat16) for k in range(far)]
    return blocks[:1] + [swap(blocks[k], "ctx", k * near) for k in range(1, far)]


def near_filters(blocks):
    me, near = lax.axis_index("ctx"), blocks[0].shape[0]
    parts = [jnp.stack([pick(b, (me % near) ^ j) for b in blocks]) for j in range(near)]
    mine = jnp.stack(parts[:1] + [swap(parts[j], "ctx", j) for j in range(1, near)])
    return mine, swap(mine, "groups", 1)


def shards(values, keys, queries, grad_out, filters):
    count = lax.axis_size("ctx")
    channels, width = values.shape
    chunk = channels // count
    twist, wave = make_tables(count, width)
    here = pl.BlockSpec(memory_space=pltpu.VMEM)
    limit = pltpu.CompilerParams(vmem_limit_bytes=24 * 1024 * 1024)
    far = 1 << ((count.bit_length() - 1) // 2)
    blocks = far_filters(filters, far)
    hbm = pl.BlockSpec(memory_space=pl.ANY)
    sent = pl.pallas_call(
        gate_kernel,
        in_specs=[hbm] * 4,
        out_specs=hbm,
        out_shape=jax.ShapeDtypeStruct((count, 2, chunk, width), jnp.bfloat16),
        scratch_shapes=[pltpu.VMEM((channels, width), jnp.bfloat16)] * 4
        + [
            pltpu.VMEM((count, 2, chunk, width), jnp.bfloat16),
            pltpu.SemaphoreType.DMA((4, STEPS)),
            pltpu.SemaphoreType.DMA((STEPS,)),
        ],
    )(values, keys, grad_out, queries)
    blocks, sent = lax.optimization_barrier((blocks, sent))
    held = exchange(sent)
    mine, other = near_filters(blocks)
    tile = min(TILE, chunk)
    tall = (count + 1) * tile
    spec = pl.pallas_call(
        filter_kernel,
        in_specs=[here] * 4,
        out_specs=here,
        out_shape=jax.ShapeDtypeStruct((chunk // tile, tall, 2 * width), jnp.bfloat16),
        scratch_shapes=[pltpu.VMEM((tall, 2 * width), jnp.bfloat16)],
        compiler_params=limit,
        cost_estimate=pl.CostEstimate(
            flops=8 * count * chunk * width * width, bytes_accessed=2**20, transcendentals=0
        ),
    )(mine, other, twist, wave)
    message = jax.ShapeDtypeStruct((3, chunk, width), jnp.bfloat16)
    made = pl.pallas_call(
        spectral_kernel,
        in_specs=[here] * 4,
        out_specs=[here] * count,
        out_shape=[message] * count,
        scratch_shapes=[
            pltpu.VMEM((count, 3, chunk, width), jnp.bfloat16),
            pltpu.VMEM((2, tall, 2 * width), jnp.bfloat16),
        ],
        compiler_params=limit,
    )(held, spec, twist, wave)
    got = spread(made)
    half = jax.ShapeDtypeStruct((channels, width), jnp.bfloat16)
    wide = jax.ShapeDtypeStruct((channels, width), jnp.float32)
    order = [0] + partners(count)
    early = max(count - WINDOW, 1)
    outs = []
    for blocks in (order[:early], order[early:]):
        outs = pl.pallas_call(
            functools.partial(ungate_kernel, blocks),
            in_specs=[here] * (3 + len(blocks)) + [hbm] * len(outs),
            out_specs=[hbm] * 4,
            out_shape=[half, half, half, wide],
            input_output_aliases={3 + len(blocks) + i: i for i in range(len(outs))},
            scratch_shapes=[pltpu.VMEM((channels, width), jnp.bfloat16)] * 3
            + [
                pltpu.VMEM((channels, width), jnp.float32),
                pltpu.SemaphoreType.DMA((4, len(blocks))),
            ],
            compiler_params=limit,
        )(values, keys, grad_out, *[got[k] for k in blocks], *outs)
    return outs


def solution(mesh):
    token = P(None, ("groups", "ctx"))
    return jax.shard_map(
        shards,
        mesh=mesh,
        in_specs=(token, token, token, token, P(None, "ctx")),
        out_specs=(token, token, token, token),
        check_vma=False,
    )
```

```python
import functools
import math

import jax
import jax.numpy as jnp
import numpy as np
from jax import lax
from jax.experimental import pallas as pl
from jax.experimental.pallas import tpu as pltpu
from jax.sharding import PartitionSpec as P

TILE = 32
STEPS = 4
WINDOW = 6
LATE = 5


def evaluate(points, theta):
    count = len(points)
    if count == 1:
        return [(theta, *points[0])]
    half, phi = count // 2, theta / 2
    c, s = math.cos(phi), math.sin(phi)
    first, second = [], []
    for (low_re, low_im), (high_re, high_im) in zip(points[:half], points[half:]):
        if theta == math.pi / 2:
            turned_re, turned_im = (high_re + high_im) * c, (high_im - high_re) * c
        else:
            turned_re, turned_im = high_re * c + high_im * s, high_im * c - high_re * s
        first.append((low_re + turned_re, low_im + turned_im))
        second.append((low_re - turned_re, low_im - turned_im))
    return evaluate(first, phi) + evaluate(second, phi + math.pi)


def interpolate(values, theta):
    count = len(values)
    if count == 1:
        return values
    half, phi = count // 2, theta / 2
    c, s = math.cos(phi), math.sin(phi)
    first = interpolate(values[:half], phi)
    second = interpolate(values[half:], phi + math.pi)
    low, high = [], []
    for (a_re, a_im), (b_re, b_im) in zip(first, second):
        gap_re, gap_im = a_re - b_re, a_im - b_im
        low.append((a_re + b_re, a_im + b_im))
        if theta == math.pi / 2:
            high.append(((gap_re - gap_im) * c, (gap_re + gap_im) * c))
        else:
            high.append((gap_re * c - gap_im * s, gap_re * s + gap_im * c))
    return low + high


def odd_values(points):
    half = len(points) // 2
    return evaluate([(low, -high) for low, high in zip(points[:half], points[half:])], math.pi / 2)


def odd_points(values):
    turned = interpolate(values, math.pi / 2)
    return [re for re, _ in turned] + [-im for _, im in turned]


def even_values(points):
    if len(points) == 2:
        return [points[0] + points[1], points[0] - points[1]]
    half = len(points) // 2
    pairs = list(zip(points[:half], points[half:]))
    return even_values([a + b for a, b in pairs]) + odd_values([a - b for a, b in pairs])


def even_points(values, count):
    if count == 2:
        return [values[0] + values[1], values[0] - values[1]]
    split = count // 4 + 1
    even, odd = even_points(values[:split], count // 2), odd_points(values[split:])
    return [a + b for a, b in zip(even, odd)] + [a - b for a, b in zip(even, odd)]


def short_values(points):
    return even_values(points) + odd_values(points)


def short_points(values, count):
    split = count // 2 + 1
    even, odd = even_points(values[:split], count), odd_points(values[split:])
    return [a + b for a, b in zip(even, odd)]


def short_angles(count):
    zero = [(0.0, 0.0)] * count
    odd = lambda n: [angle for angle, *_ in evaluate(zero[: n // 2], math.pi / 2)]
    sizes, even = [count], count
    while even > 2:
        even //= 2
        sizes.append(even)
    return [0.0, math.pi] + sum((odd(n) for n in reversed(sizes)), [])


def make_tables(count, width):
    angles = np.array(short_angles(count))
    turn = np.outer(angles, np.arange(width)) / width
    scale = np.where(np.arange(len(angles)) < 2, 1.0, 2.0)[:, None] / (2 * count * width)
    twist = np.stack(
        [np.cos(turn), np.sin(turn), np.cos(turn) * scale, np.sin(turn) * scale], axis=1
    ).astype(np.float32)
    wave = np.outer(np.arange(width), np.arange(width)) % width * (2 * math.pi / width)
    c, s = np.cos(wave), np.sin(wave)
    ahead = np.block([[c, -s], [s, c]])
    return twist, jnp.asarray(np.stack([ahead, ahead.T]), jnp.bfloat16)


def rows_of(block, chunk):
    return pl.ds(pl.multiple_of(block * chunk, chunk), chunk)


def gate_kernel(value_hbm, key_hbm, cot_hbm, query_hbm, out_hbm, *scratch):
    blocks, _, chunk, width = out_hbm.shape
    sources = (value_hbm, key_hbm, cot_hbm, query_hbm)
    *held, made, loads, stores = scratch
    span, some = blocks * chunk // STEPS, blocks // STEPS
    copies = []
    for step in range(STEPS):
        rows = pl.ds(step * span, span)
        copies.append(
            [
                pltpu.make_async_copy(source.at[rows], to.at[rows], loads.at[i, step])
                for i, (source, to) in enumerate(zip(sources, held))
            ]
        )
        for copy in copies[-1]:
            copy.start()
    sends = []
    for step in range(STEPS):
        for copy in copies[step]:
            copy.wait()
        rows, part = pl.ds(step * span, span), pl.ds(step * some, some)
        for which in range(2):
            left, right = held[2 * which][rows], held[2 * which + 1][rows]
            both = left.astype(jnp.float32) * right.astype(jnp.float32)
            made[part, which] = both.astype(jnp.bfloat16).reshape(some, chunk, width)
        sends.append(pltpu.make_async_copy(made.at[part], out_hbm.at[part], stores.at[step]))
        sends[-1].start()
    for send in sends:
        send.wait()


def transform(points, twist_ref, wave_ref, turned_ref):
    tile, width = points[0].shape
    points = [point.astype(jnp.float32) for point in points]
    for top in range(0, tile, 16):
        halves = []
        for start in (top, top + 8):
            done = []
            for k, value in enumerate(short_values([p[start : start + 8] for p in points])):
                c, s = twist_ref[k, 0:1, :], twist_ref[k, 1:2, :]
                if k == 0:
                    re, im = value, jnp.zeros_like(value)
                elif k == 1:
                    re, im = value * c, value * -s
                else:
                    _, re, im = value
                    re, im = re * c + im * s, im * c - re * s
                done.append((re, im))
            halves.append(done)
        for k, ((a_re, a_im), (b_re, b_im)) in enumerate(zip(*halves)):
            rows = slice(k * tile + top, k * tile + top + 16)
            turned_ref[rows, :width] = jnp.concatenate([a_re, b_re]).astype(jnp.bfloat16)
            turned_ref[rows, width:] = jnp.concatenate([a_im, b_im]).astype(jnp.bfloat16)
    return jnp.dot(turned_ref[...], wave_ref[0], preferred_element_type=jnp.float32)


def inverse(re, im, twist_ref, wave_ref):
    count, _, width = twist_ref.shape
    tile = re.shape[0] // count
    both = jnp.concatenate([re.astype(jnp.bfloat16), im.astype(jnp.bfloat16)], axis=1)
    back = jnp.dot(both, wave_ref[1], preferred_element_type=jnp.float32)
    parts = []
    for start in range(0, tile, 8):
        values = []
        for k in range(count):
            rows = slice(k * tile + start, k * tile + start + 8)
            re, im = back[rows, :width], back[rows, width:]
            c, s = twist_ref[k, 2:3, :], twist_ref[k, 3:4, :]
            if k == 0:
                values.append(re * c)
            elif k == 1:
                values.append(re * c - im * s)
            else:
                values.append((re * c - im * s, re * s + im * c))
        parts.append(short_points(values, count - 1))
    return [jnp.concatenate(part) for part in zip(*parts)]


def filter_kernel(mine_ref, other_ref, twist_ref, wave_ref, spec_ref, turned_ref):
    near, far, rows, _ = mine_ref.shape
    tile = spec_ref.shape[1] // twist_ref.shape[0]
    me, side = lax.axis_index("ctx"), lax.axis_index("groups")

    def piece(share_ref, b, lanes):
        return share_ref[(me % near) ^ (b % near), (me // near) ^ (b // near), lanes]

    def points(first, lanes):
        return [
            jnp.where(side == first, piece(mine_ref, b, lanes), piece(other_ref, b, lanes))
            for b in range(near * far)
        ]

    if rows < tile:
        parts = zip(*[points(half, slice(None)) for half in range(2)])
        joined = [jnp.concatenate([p.astype(jnp.float32) for p in pair]) for pair in parts]
        spec = transform(joined, twist_ref, wave_ref, turned_ref)
        spec_ref[0] = spec.astype(jnp.bfloat16)
    else:
        for half in range(2):

            @pl.loop(0, rows // tile)
            def _(step):
                lanes = pl.ds(pl.multiple_of(step * tile, tile), tile)
                spec = transform(points(half, lanes), twist_ref, wave_ref, turned_ref)
                spec_ref[half * (rows // tile) + step] = spec.astype(jnp.bfloat16)


def spectral_kernel(sig_ref, spec_ref, twist_ref, wave_ref, *refs):
    *out_refs, made_ref, turned_ref = refs
    count, _, chunk, width = sig_ref.shape
    tile = spec_ref.shape[1] // twist_ref.shape[0]
    me, steps = lax.axis_index("ctx"), chunk // tile

    def deliver(step):
        lanes = rows_of(step, tile)
        for k in range(count):
            out_refs[k][:, lanes] = made_ref[k, :, lanes]

    @pl.loop(0, steps)
    def _(step):
        deliver(jnp.maximum(step - 1, 0))
        lanes = rows_of(step, tile)
        specs = []
        for which in range(2):
            points = [sig_ref[b, which, lanes] for b in range(count)]
            spec = transform(points, twist_ref, wave_ref, turned_ref.at[which])
            specs.append((spec[:, :width], spec[:, width:]))
        (m_re, m_im), (g_re, g_im) = specs
        spec = spec_ref[step].astype(jnp.float32)
        f_re, f_im = spec[:, :width], spec[:, width:]
        results = (
            (f_re * m_re - f_im * m_im, f_re * m_im + f_im * m_re),
            (f_re * g_re + f_im * g_im, f_re * g_im - f_im * g_re),
            (g_re * m_re + g_im * m_im, g_im * m_re - g_re * m_im),
        )
        for which, (re, im) in enumerate(results):
            for b, part in enumerate(inverse(re, im, twist_ref, wave_ref)):
                made_ref[me ^ b, which, lanes] = part.astype(jnp.bfloat16)

    deliver(steps - 1)


def gates(operands, part_ref, made, rows):
    value, key, cot = (operand.astype(jnp.float32) for operand in operands)
    conv, grad, filt = (part_ref[which].astype(jnp.float32) for which in range(3))
    made[0][rows] = (grad * key).astype(jnp.bfloat16)
    made[1][rows] = (grad * value).astype(jnp.bfloat16)
    made[2][rows] = (cot * conv).astype(jnp.bfloat16)
    made[3][rows] = filt


def send_rows(made, outs, rows, sems, i):
    sends = [
        pltpu.make_async_copy(source.at[rows], to.at[rows], sems.at[j, i])
        for j, (source, to) in enumerate(zip(made, outs))
    ]
    for send in sends:
        send.start()
    return sends


def first_gates(early, late, *refs):
    operands, part_refs = refs[:3], refs[3 : 3 + len(early)]
    *outs, late_ref = refs[3 + len(early) : 8 + len(early)]
    held_ref, *made, loads, stores = refs[8 + len(early) :]
    me = lax.axis_index("ctx")
    copies = []
    for i, k in enumerate(early + late):
        rows = rows_of(me ^ k, part_refs[0].shape[1])
        to = held_ref.at[i] if i < len(early) else late_ref.at[i - len(early)]
        copies.append(
            [
                pltpu.make_async_copy(operand.at[rows], to.at[j], loads.at[j, i])
                for j, operand in enumerate(operands)
            ]
        )
        for copy in copies[-1]:
            copy.start()
    sends = []
    for i, k in enumerate(early):
        for copy in copies[i]:
            copy.wait()
        rows = rows_of(me ^ k, part_refs[0].shape[1])
        gates([held_ref[i, j] for j in range(3)], part_refs[i], made, rows)
        sends += send_rows(made, outs, rows, stores, i)
    for copy in sum(copies[len(early) :], []) + sends:
        copy.wait()


def last_gates(late, held_ref, *refs):
    part_refs, outs = refs[: len(late)], refs[len(late) + 4 : len(late) + 8]
    *made, stores = refs[len(late) + 8 :]
    me = lax.axis_index("ctx")
    sends = []
    for i, k in enumerate(late):
        rows = rows_of(me ^ k, part_refs[0].shape[1])
        gates([held_ref[i, j] for j in range(3)], part_refs[i], made, rows)
        sends += send_rows(made, outs, rows, stores, i)
    for send in sends:
        send.wait()


def partners(count):
    near, size = [], count // 4
    while size:
        near += range(size, 2 * size)
        size //= 2
    far = list(range(count // 2, count))
    order = []
    for i, k in enumerate(far):
        order += [k] + near[i : i + 1]
    return order


def spread(blocks):
    count = len(blocks)
    got = list(blocks)
    order = partners(count)
    for i, k in enumerate(order):
        block = blocks[k]
        if i >= WINDOW:
            before = order[i - WINDOW]
            block, got[before] = lax.optimization_barrier((block, got[before]))
        got[k] = lax.ppermute(block, "ctx", [(j, j ^ k) for j in range(count)])
    return got


def exchange(parts):
    return lax.all_to_all(parts, "ctx", split_axis=0, concat_axis=0, tiled=True)


def swap(block, axis, gap):
    size = lax.axis_size(axis)
    return lax.ppermute(block, axis, [(i, i ^ gap) for i in range(size)])


def pick(blocks, where):
    return lax.dynamic_index_in_dim(blocks, where, 0, keepdims=False)


def far_filters(filters, far):
    count, me, side = lax.axis_size("ctx"), lax.axis_index("ctx"), lax.axis_index("groups")
    near = count // far
    channels, width = filters.shape
    share = filters.reshape(far, near, 2, channels // count // 2, width)
    share = lax.dynamic_index_in_dim(share, side, 2, keepdims=False)
    blocks = [pick(share, (me // near) ^ k).astype(jnp.bfloat16) for k in range(far)]
    return blocks[:1] + [swap(blocks[k], "ctx", k * near) for k in range(1, far)]


def near_filters(blocks):
    me, near = lax.axis_index("ctx"), blocks[0].shape[0]
    parts = [jnp.stack([pick(b, (me % near) ^ j) for b in blocks]) for j in range(near)]
    mine = jnp.stack(parts[:1] + [swap(parts[j], "ctx", j) for j in range(1, near)])
    return mine, swap(mine, "groups", 1)


def shards(values, keys, queries, grad_out, filters):
    count = lax.axis_size("ctx")
    channels, width = values.shape
    chunk = channels // count
    twist, wave = make_tables(count, width)
    here = pl.BlockSpec(memory_space=pltpu.VMEM)
    limit = pltpu.CompilerParams(vmem_limit_bytes=24 * 1024 * 1024)
    far = 1 << ((count.bit_length() - 1) // 2)
    blocks = far_filters(filters, far)
    hbm = pl.BlockSpec(memory_space=pl.ANY)
    sent = pl.pallas_call(
        gate_kernel,
        in_specs=[hbm] * 4,
        out_specs=hbm,
        out_shape=jax.ShapeDtypeStruct((count, 2, chunk, width), jnp.bfloat16),
        scratch_shapes=[pltpu.VMEM((channels, width), jnp.bfloat16)] * 4
        + [
            pltpu.VMEM((count, 2, chunk, width), jnp.bfloat16),
            pltpu.SemaphoreType.DMA((4, STEPS)),
            pltpu.SemaphoreType.DMA((STEPS,)),
        ],
    )(values, keys, grad_out, queries)
    blocks, sent = lax.optimization_barrier((blocks, sent))
    held = exchange(sent)
    mine, other = near_filters(blocks)
    tile = min(TILE, chunk)
    tall = (count + 1) * tile
    spec = pl.pallas_call(
        filter_kernel,
        in_specs=[here] * 4,
        out_specs=here,
        out_shape=jax.ShapeDtypeStruct((chunk // tile, tall, 2 * width), jnp.bfloat16),
        scratch_shapes=[pltpu.VMEM((tall, 2 * width), jnp.bfloat16)],
        compiler_params=limit,
        cost_estimate=pl.CostEstimate(
            flops=8 * count * chunk * width * width, bytes_accessed=2**20, transcendentals=0
        ),
    )(mine, other, twist, wave)
    message = jax.ShapeDtypeStruct((3, chunk, width), jnp.bfloat16)
    made = pl.pallas_call(
        spectral_kernel,
        in_specs=[here] * 4,
        out_specs=[here] * count,
        out_shape=[message] * count,
        scratch_shapes=[
            pltpu.VMEM((count, 3, chunk, width), jnp.bfloat16),
            pltpu.VMEM((2, tall, 2 * width), jnp.bfloat16),
        ],
        compiler_params=limit,
    )(held, spec, twist, wave)
    got = spread(made)
    half = jax.ShapeDtypeStruct((channels, width), jnp.bfloat16)
    wide = jax.ShapeDtypeStruct((channels, width), jnp.float32)
    order = [0] + partners(count)
    early, late = order[:-LATE], order[-LATE:]
    made_scratch = [pltpu.VMEM((channels, width), jnp.bfloat16)] * 3 + [
        pltpu.VMEM((channels, width), jnp.float32)
    ]
    *outs, operands = pl.pallas_call(
        functools.partial(first_gates, early, late),
        in_specs=[hbm] * 3 + [here] * len(early),
        out_specs=[hbm] * 4 + [here],
        out_shape=[half] * 3
        + [wide, jax.ShapeDtypeStruct((len(late), 3, chunk, width), jnp.bfloat16)],
        scratch_shapes=[
            pltpu.VMEM((len(early), 3, chunk, width), jnp.bfloat16),
            *made_scratch,
            pltpu.SemaphoreType.DMA((3, count)),
            pltpu.SemaphoreType.DMA((4, len(early))),
        ],
        compiler_params=pltpu.CompilerParams(vmem_limit_bytes=24 * 1024 * 1024),
    )(values, keys, grad_out, *[got[k] for k in early])
    return pl.pallas_call(
        functools.partial(last_gates, late),
        in_specs=[here] * (1 + len(late)) + [hbm] * 4,
        out_specs=[hbm] * 4,
        out_shape=[half] * 3 + [wide],
        input_output_aliases={1 + len(late) + i: i for i in range(4)},
        scratch_shapes=[*made_scratch, pltpu.SemaphoreType.DMA((4, len(late)))],
        compiler_params=limit,
    )(operands, *[got[k] for k in late], *outs)


def solution(mesh):
    token = P(None, ("groups", "ctx"))
    return jax.shard_map(
        shards,
        mesh=mesh,
        in_specs=(token, token, token, token, P(None, "ctx")),
        out_specs=(token, token, token, token),
        check_vma=False,
    )
```

```python
import functools
import math

import jax
import jax.numpy as jnp
import numpy as np
from jax import lax
from jax.experimental import pallas as pl
from jax.experimental.pallas import tpu as pltpu
from jax.sharding import PartitionSpec as P

TILE = 16
GROUP = 4
STEPS = 4
WINDOW = 6
LATE = 5


def evaluate(points, theta):
    count = len(points)
    if count == 1:
        return [(theta, *points[0])]
    half, phi = count // 2, theta / 2
    c, s = math.cos(phi), math.sin(phi)
    first, second = [], []
    for (low_re, low_im), (high_re, high_im) in zip(points[:half], points[half:]):
        if theta == math.pi / 2:
            turned_re, turned_im = (high_re + high_im) * c, (high_im - high_re) * c
        else:
            turned_re, turned_im = high_re * c + high_im * s, high_im * c - high_re * s
        first.append((low_re + turned_re, low_im + turned_im))
        second.append((low_re - turned_re, low_im - turned_im))
    return evaluate(first, phi) + evaluate(second, phi + math.pi)


def interpolate(values, theta):
    count = len(values)
    if count == 1:
        return values
    half, phi = count // 2, theta / 2
    c, s = math.cos(phi), math.sin(phi)
    first = interpolate(values[:half], phi)
    second = interpolate(values[half:], phi + math.pi)
    low, high = [], []
    for (a_re, a_im), (b_re, b_im) in zip(first, second):
        gap_re, gap_im = a_re - b_re, a_im - b_im
        low.append((a_re + b_re, a_im + b_im))
        if theta == math.pi / 2:
            high.append(((gap_re - gap_im) * c, (gap_re + gap_im) * c))
        else:
            high.append((gap_re * c - gap_im * s, gap_re * s + gap_im * c))
    return low + high


def odd_values(points):
    half = len(points) // 2
    return evaluate([(low, -high) for low, high in zip(points[:half], points[half:])], math.pi / 2)


def odd_points(values):
    turned = interpolate(values, math.pi / 2)
    return [re for re, _ in turned] + [-im for _, im in turned]


def even_values(points):
    if len(points) == 2:
        return [points[0] + points[1], points[0] - points[1]]
    half = len(points) // 2
    pairs = list(zip(points[:half], points[half:]))
    return even_values([a + b for a, b in pairs]) + odd_values([a - b for a, b in pairs])


def even_points(values, count):
    if count == 2:
        return [values[0] + values[1], values[0] - values[1]]
    split = count // 4 + 1
    even, odd = even_points(values[:split], count // 2), odd_points(values[split:])
    return [a + b for a, b in zip(even, odd)] + [a - b for a, b in zip(even, odd)]


def short_values(points):
    return even_values(points) + odd_values(points)


def short_points(values, count):
    split = count // 2 + 1
    even, odd = even_points(values[:split], count), odd_points(values[split:])
    return [a + b for a, b in zip(even, odd)]


def short_angles(count):
    zero = [(0.0, 0.0)] * count
    odd = lambda n: [angle for angle, *_ in evaluate(zero[: n // 2], math.pi / 2)]
    sizes, even = [count], count
    while even > 2:
        even //= 2
        sizes.append(even)
    return [0.0, math.pi] + sum((odd(n) for n in reversed(sizes)), [])


def make_tables(count, width, tile):
    angles = np.array(short_angles(count))
    turn = np.outer(angles, np.arange(width)) / width
    scale = np.where(np.arange(len(angles)) < 2, 1.0, 2.0)[:, None] / (2 * count * width)
    twist = np.stack(
        [np.cos(turn), np.sin(turn), np.cos(turn) * scale, np.sin(turn) * scale], axis=1
    ).astype(np.float32)
    wave = np.outer(np.arange(width), np.arange(width)) % width * (2 * math.pi / width)
    c, s = np.cos(wave), np.sin(wave)
    ahead = np.block([[c, -s], [s, c]])
    short = np.zeros((2, 1, 1))
    if on_matrix_unit(count, tile):
        turn = np.outer(angles, np.arange(count))
        parts = np.stack([np.cos(turn), -np.sin(turn)], axis=1)
        parts = np.concatenate([parts[:2, 0], parts[2:].reshape(-1, count)])
        short = np.kron(parts, np.eye(tile)).reshape(2, count * tile, count * tile)
    waves = np.stack([ahead, ahead.T])
    return twist, jnp.asarray(waves, jnp.bfloat16), jnp.asarray(short, jnp.bfloat16)


def on_matrix_unit(count, tile):
    return count * tile <= 256


def rows_of(block, chunk):
    return pl.ds(pl.multiple_of(block * chunk, chunk), chunk)


def gate_kernel(value_hbm, key_hbm, cot_hbm, query_hbm, out_hbm, *scratch):
    blocks, _, chunk, width = out_hbm.shape
    sources = (value_hbm, key_hbm, cot_hbm, query_hbm)
    *held, made, loads, stores = scratch
    span, some = blocks * chunk // STEPS, blocks // STEPS
    copies = []
    for step in range(STEPS):
        rows = pl.ds(step * span, span)
        copies.append(
            [
                pltpu.make_async_copy(source.at[rows], to.at[rows], loads.at[i, step])
                for i, (source, to) in enumerate(zip(sources, held))
            ]
        )
        for copy in copies[-1]:
            copy.start()
    sends = []
    for step in range(STEPS):
        for copy in copies[step]:
            copy.wait()
        rows, part = pl.ds(step * span, span), pl.ds(step * some, some)
        for which in range(2):
            left, right = held[2 * which][rows], held[2 * which + 1][rows]
            both = left.astype(jnp.float32) * right.astype(jnp.float32)
            made[part, which] = both.astype(jnp.bfloat16).reshape(some, chunk, width)
        sends.append(pltpu.make_async_copy(made.at[part], out_hbm.at[part], stores.at[step]))
        sends[-1].start()
    for send in sends:
        send.wait()


def short_stage(blocks, short_ref):
    count, (tile, width) = len(blocks[0]), blocks[0][0].shape
    if not on_matrix_unit(count, tile):
        blocks = [[b.astype(jnp.float32) for b in points] for points in blocks]
        values = [short_values(points) for points in blocks]
        return [v[:2] + [(re, im) for _, re, im in v[2:]] for v in values]
    side = jnp.concatenate([jnp.concatenate(points) for points in blocks], axis=1)
    parts = jnp.concatenate(
        [jnp.dot(short_ref[i], side, preferred_element_type=jnp.float32) for i in range(2)]
    )

    def part(i, which):
        return parts[i * tile : (i + 1) * tile, which * width : (which + 1) * width]

    return [
        [part(0, which), part(1, which)]
        + [(part(2 * k - 2, which), part(2 * k - 1, which)) for k in range(2, count + 1)]
        for which in range(len(blocks))
    ]


def transform(blocks, twist_ref, wave_ref, short_ref, turned_ref):
    tile, width = blocks[0][0].shape
    tall = (len(blocks[0]) + 1) * tile
    for which, values in enumerate(short_stage(blocks, short_ref)):
        for k, value in enumerate(values):
            c, s = twist_ref[k, 0:1, :], twist_ref[k, 1:2, :]
            if k == 0:
                re, im = value, jnp.zeros_like(value)
            elif k == 1:
                re, im = value * c, value * -s
            else:
                re, im = value[0] * c + value[1] * s, value[1] * c - value[0] * s
            rows = slice(which * tall + k * tile, which * tall + (k + 1) * tile)
            turned_ref[rows, :width] = re.astype(jnp.bfloat16)
            turned_ref[rows, width:] = im.astype(jnp.bfloat16)
    turned = turned_ref[: len(blocks) * tall]
    spec = jnp.dot(turned, wave_ref[0], preferred_element_type=jnp.float32)
    return [spec[which * tall : (which + 1) * tall] for which in range(len(blocks))]


def inverse(re, im, twist_ref, wave_ref):
    count, _, width = twist_ref.shape
    tile = re.shape[0] // count
    both = jnp.concatenate([re.astype(jnp.bfloat16), im.astype(jnp.bfloat16)], axis=1)
    back = jnp.dot(both, wave_ref[1], preferred_element_type=jnp.float32)
    parts = []
    for start in range(0, tile, 8):
        values = []
        for k in range(count):
            rows = slice(k * tile + start, k * tile + start + 8)
            re, im = back[rows, :width], back[rows, width:]
            c, s = twist_ref[k, 2:3, :], twist_ref[k, 3:4, :]
            if k == 0:
                values.append(re * c)
            elif k == 1:
                values.append(re * c - im * s)
            else:
                values.append((re * c - im * s, re * s + im * c))
        parts.append(short_points(values, count - 1))
    return [jnp.concatenate(part) for part in zip(*parts)]


def filter_kernel(mine_ref, other_ref, twist_ref, wave_ref, short_ref, spec_ref, turned_ref):
    near, far, rows, _ = mine_ref.shape
    tile = spec_ref.shape[1] // twist_ref.shape[0]
    me, side = lax.axis_index("ctx"), lax.axis_index("groups")
    for first, table in ((4, wave_ref), (2, short_ref)):
        for i in range(2):
            _, high, wide = table.shape
            spec_ref[spec_ref.shape[0] - first + i, :high, :wide] = table[i]

    def piece(share_ref, b, lanes):
        return share_ref[(me % near) ^ (b % near), (me // near) ^ (b // near), lanes]

    def points(first, lanes):
        return [
            jnp.where(side == first, piece(mine_ref, b, lanes), piece(other_ref, b, lanes))
            for b in range(near * far)
        ]

    if rows < tile:
        parts = zip(*[points(half, slice(None)) for half in range(2)])
        joined = [jnp.concatenate([p.astype(jnp.float32) for p in pair]) for pair in parts]
        (spec,) = transform([joined], twist_ref, wave_ref, short_ref, turned_ref)
        spec_ref[0] = spec.astype(jnp.bfloat16)
        return
    group = turned_ref.shape[0] // spec_ref.shape[1] // 2

    @pl.loop(0, rows // tile // group)
    def _(step):
        tiles = [step * group + t for t in range(group)]
        blocks = [points(half, rows_of(t, tile)) for half in range(2) for t in tiles]
        specs = transform(blocks, twist_ref, wave_ref, short_ref, turned_ref)
        for i, spec in enumerate(specs):
            half, t = i // group, tiles[i % group]
            spec_ref[half * (rows // tile) + t] = spec.astype(jnp.bfloat16)


def spectral_kernel(sig_ref, spec_ref, twist_ref, *refs):
    *out_refs, made_ref, turned_ref = refs
    count, _, chunk, width = sig_ref.shape
    tile = spec_ref.shape[1] // twist_ref.shape[0]
    group = turned_ref.shape[0] // spec_ref.shape[1] // 2
    me, steps = lax.axis_index("ctx"), chunk // tile // group
    size = count * tile if on_matrix_unit(count, tile) else 1
    wave_ref = spec_ref.at[chunk // tile : chunk // tile + 2, : 2 * width]
    short_ref = spec_ref.at[chunk // tile + 2 :, :size, :size]

    def deliver(step):
        lanes = rows_of(step, tile * group)
        for k in range(count):
            out_refs[k][:, lanes] = made_ref[k, :, lanes]

    @pl.loop(0, steps)
    def _(step):
        deliver(jnp.maximum(step - 1, 0))
        tiles = [step * group + t for t in range(group)]
        blocks = [
            [sig_ref[b, which, rows_of(t, tile)] for b in range(count)]
            for t in tiles
            for which in range(2)
        ]
        both = transform(blocks, twist_ref, wave_ref, short_ref, turned_ref)
        for i, t in enumerate(tiles):
            specs = [*both[2 * i : 2 * i + 2], spec_ref[t].astype(jnp.float32)]
            (m_re, m_im), (g_re, g_im), (f_re, f_im) = ((s[:, :width], s[:, width:]) for s in specs)
            results = (
                (f_re * m_re - f_im * m_im, f_re * m_im + f_im * m_re),
                (f_re * g_re + f_im * g_im, f_re * g_im - f_im * g_re),
                (g_re * m_re + g_im * m_im, g_im * m_re - g_re * m_im),
            )
            for which, (re, im) in enumerate(results):
                for b, part in enumerate(inverse(re, im, twist_ref, wave_ref)):
                    made_ref[me ^ b, which, rows_of(t, tile)] = part.astype(jnp.bfloat16)

    deliver(steps - 1)


def gates(operands, part_ref, made, rows):
    value, key, cot = (operand.astype(jnp.float32) for operand in operands)
    conv, grad, filt = (part_ref[which].astype(jnp.float32) for which in range(3))
    made[0][rows] = (grad * key).astype(jnp.bfloat16)
    made[1][rows] = (grad * value).astype(jnp.bfloat16)
    made[2][rows] = (cot * conv).astype(jnp.bfloat16)
    made[3][rows] = filt


def send_rows(made, outs, rows, sems, i):
    sends = [
        pltpu.make_async_copy(source.at[rows], to.at[rows], sems.at[j, i])
        for j, (source, to) in enumerate(zip(made, outs))
    ]
    for send in sends:
        send.start()
    return sends


def first_gates(early, late, *refs):
    operands, part_refs = refs[:3], refs[3 : 3 + len(early)]
    *outs, late_ref = refs[3 + len(early) : 8 + len(early)]
    held_ref, *made, loads, stores = refs[8 + len(early) :]
    me = lax.axis_index("ctx")
    copies = []
    for i, k in enumerate(early + late):
        rows = rows_of(me ^ k, part_refs[0].shape[1])
        to = held_ref.at[i] if i < len(early) else late_ref.at[i - len(early)]
        copies.append(
            [
                pltpu.make_async_copy(operand.at[rows], to.at[j], loads.at[j, i])
                for j, operand in enumerate(operands)
            ]
        )
        for copy in copies[-1]:
            copy.start()
    sends = []
    for i, k in enumerate(early):
        for copy in copies[i]:
            copy.wait()
        rows = rows_of(me ^ k, part_refs[0].shape[1])
        gates([held_ref[i, j] for j in range(3)], part_refs[i], made, rows)
        sends += send_rows(made, outs, rows, stores, i)
    for copy in sum(copies[len(early) :], []) + sends:
        copy.wait()


def last_gates(late, held_ref, *refs):
    part_refs, outs = refs[: len(late)], refs[len(late) + 4 : len(late) + 8]
    *made, stores = refs[len(late) + 8 :]
    me = lax.axis_index("ctx")
    sends = []
    for i, k in enumerate(late):
        rows = rows_of(me ^ k, part_refs[0].shape[1])
        gates([held_ref[i, j] for j in range(3)], part_refs[i], made, rows)
        sends += send_rows(made, outs, rows, stores, i)
    for send in sends:
        send.wait()


def partners(count):
    near, size = [], count // 4
    while size:
        near += range(size, 2 * size)
        size //= 2
    far = list(range(count // 2, count))
    order = []
    for i, k in enumerate(far):
        order += [k] + near[i : i + 1]
    return order


def spread(blocks):
    count = len(blocks)
    got = list(blocks)
    order = partners(count)
    for i, k in enumerate(order):
        block = blocks[k]
        if i >= WINDOW:
            before = order[i - WINDOW]
            block, got[before] = lax.optimization_barrier((block, got[before]))
        got[k] = lax.ppermute(block, "ctx", [(j, j ^ k) for j in range(count)])
    return got


def exchange(parts):
    return lax.all_to_all(parts, "ctx", split_axis=0, concat_axis=0, tiled=True)


def swap(block, axis, gap):
    size = lax.axis_size(axis)
    return lax.ppermute(block, axis, [(i, i ^ gap) for i in range(size)])


def pick(blocks, where):
    return lax.dynamic_index_in_dim(blocks, where, 0, keepdims=False)


def far_filters(filters, far):
    count, me, side = lax.axis_size("ctx"), lax.axis_index("ctx"), lax.axis_index("groups")
    near = count // far
    channels, width = filters.shape
    share = filters.reshape(far, near, 2, channels // count // 2, width)
    share = lax.dynamic_index_in_dim(share, side, 2, keepdims=False)
    blocks = [pick(share, (me // near) ^ k).astype(jnp.bfloat16) for k in range(far)]
    return blocks[:1] + [swap(blocks[k], "ctx", k * near) for k in range(1, far)]


def near_filters(blocks):
    me, near = lax.axis_index("ctx"), blocks[0].shape[0]
    parts = [jnp.stack([pick(b, (me % near) ^ j) for b in blocks]) for j in range(near)]
    mine = jnp.stack(parts[:1] + [swap(parts[j], "ctx", j) for j in range(1, near)])
    return mine, swap(mine, "groups", 1)


def shards(values, keys, queries, grad_out, filters):
    count = lax.axis_size("ctx")
    channels, width = values.shape
    chunk = channels // count
    tile = min(TILE, chunk)
    twist, wave, short = make_tables(count, width, tile)
    here = pl.BlockSpec(memory_space=pltpu.VMEM)
    limit = pltpu.CompilerParams(vmem_limit_bytes=24 * 1024 * 1024)
    far = 1 << ((count.bit_length() - 1) // 2)
    blocks = far_filters(filters, far)
    hbm = pl.BlockSpec(memory_space=pl.ANY)
    sent = pl.pallas_call(
        gate_kernel,
        in_specs=[hbm] * 4,
        out_specs=hbm,
        out_shape=jax.ShapeDtypeStruct((count, 2, chunk, width), jnp.bfloat16),
        scratch_shapes=[pltpu.VMEM((channels, width), jnp.bfloat16)] * 4
        + [
            pltpu.VMEM((count, 2, chunk, width), jnp.bfloat16),
            pltpu.SemaphoreType.DMA((4, STEPS)),
            pltpu.SemaphoreType.DMA((STEPS,)),
        ],
    )(values, keys, grad_out, queries)
    blocks, sent = lax.optimization_barrier((blocks, sent))
    held = exchange(sent)
    mine, other = near_filters(blocks)
    group = min(GROUP, chunk // tile)
    tall = (count + 1) * tile
    spec = pl.pallas_call(
        filter_kernel,
        in_specs=[here] * 5,
        out_specs=here,
        out_shape=jax.ShapeDtypeStruct((chunk // tile + 4, tall, 2 * width), jnp.bfloat16),
        scratch_shapes=[pltpu.VMEM((2 * max(group // 2, 1) * tall, 2 * width), jnp.bfloat16)],
        compiler_params=limit,
        cost_estimate=pl.CostEstimate(
            flops=8 * count * chunk * width * width, bytes_accessed=2**20, transcendentals=0
        ),
    )(mine, other, twist, wave, short)
    message = jax.ShapeDtypeStruct((3, chunk, width), jnp.bfloat16)
    made = pl.pallas_call(
        spectral_kernel,
        in_specs=[here] * 3,
        out_specs=[here] * count,
        out_shape=[message] * count,
        scratch_shapes=[
            pltpu.VMEM((count, 3, chunk, width), jnp.bfloat16),
            pltpu.VMEM((2 * group * tall, 2 * width), jnp.bfloat16),
        ],
        compiler_params=limit,
    )(held, spec, twist)
    got = spread(made)
    half = jax.ShapeDtypeStruct((channels, width), jnp.bfloat16)
    wide = jax.ShapeDtypeStruct((channels, width), jnp.float32)
    order = [0] + partners(count)
    early, late = order[:-LATE], order[-LATE:]
    made_scratch = [pltpu.VMEM((channels, width), jnp.bfloat16)] * 3 + [
        pltpu.VMEM((channels, width), jnp.float32)
    ]
    *outs, operands = pl.pallas_call(
        functools.partial(first_gates, early, late),
        in_specs=[hbm] * 3 + [here] * len(early),
        out_specs=[hbm] * 4 + [here],
        out_shape=[half] * 3
        + [wide, jax.ShapeDtypeStruct((len(late), 3, chunk, width), jnp.bfloat16)],
        scratch_shapes=[
            pltpu.VMEM((len(early), 3, chunk, width), jnp.bfloat16),
            *made_scratch,
            pltpu.SemaphoreType.DMA((3, count)),
            pltpu.SemaphoreType.DMA((4, len(early))),
        ],
        compiler_params=pltpu.CompilerParams(vmem_limit_bytes=24 * 1024 * 1024),
    )(values, keys, grad_out, *[got[k] for k in early])
    return pl.pallas_call(
        functools.partial(last_gates, late),
        in_specs=[here] * (1 + len(late)) + [hbm] * 4,
        out_specs=[hbm] * 4,
        out_shape=[half] * 3 + [wide],
        input_output_aliases={1 + len(late) + i: i for i in range(4)},
        scratch_shapes=[*made_scratch, pltpu.SemaphoreType.DMA((4, len(late)))],
        compiler_params=limit,
    )(operands, *[got[k] for k in late], *outs)


def solution(mesh):
    token = P(None, ("groups", "ctx"))
    return jax.shard_map(
        shards,
        mesh=mesh,
        in_specs=(token, token, token, token, P(None, "ctx")),
        out_specs=(token, token, token, token),
        check_vma=False,
    )
```

```python
import functools
import math

import jax
import jax.numpy as jnp
import numpy as np
from jax import lax
from jax.experimental import pallas as pl
from jax.experimental.pallas import tpu as pltpu
from jax.sharding import PartitionSpec as P

TILE = 16
GROUP = 4
ON_UNIT = 2
STEPS = 4
WINDOW = 6
LATE = 5


def evaluate(points, theta):
    count = len(points)
    if count == 1:
        return [(theta, *points[0])]
    half, phi = count // 2, theta / 2
    c, s = math.cos(phi), math.sin(phi)
    first, second = [], []
    for (low_re, low_im), (high_re, high_im) in zip(points[:half], points[half:]):
        if theta == math.pi / 2:
            turned_re, turned_im = (high_re + high_im) * c, (high_im - high_re) * c
        else:
            turned_re, turned_im = high_re * c + high_im * s, high_im * c - high_re * s
        first.append((low_re + turned_re, low_im + turned_im))
        second.append((low_re - turned_re, low_im - turned_im))
    return evaluate(first, phi) + evaluate(second, phi + math.pi)


def interpolate(values, theta):
    count = len(values)
    if count == 1:
        return values
    half, phi = count // 2, theta / 2
    c, s = math.cos(phi), math.sin(phi)
    first = interpolate(values[:half], phi)
    second = interpolate(values[half:], phi + math.pi)
    low, high = [], []
    for (a_re, a_im), (b_re, b_im) in zip(first, second):
        gap_re, gap_im = a_re - b_re, a_im - b_im
        low.append((a_re + b_re, a_im + b_im))
        if theta == math.pi / 2:
            high.append(((gap_re - gap_im) * c, (gap_re + gap_im) * c))
        else:
            high.append((gap_re * c - gap_im * s, gap_re * s + gap_im * c))
    return low + high


def odd_values(points):
    half = len(points) // 2
    return evaluate([(low, -high) for low, high in zip(points[:half], points[half:])], math.pi / 2)


def odd_points(values):
    turned = interpolate(values, math.pi / 2)
    return [re for re, _ in turned] + [-im for _, im in turned]


def even_values(points):
    if len(points) == 2:
        return [points[0] + points[1], points[0] - points[1]]
    half = len(points) // 2
    pairs = list(zip(points[:half], points[half:]))
    return even_values([a + b for a, b in pairs]) + odd_values([a - b for a, b in pairs])


def even_points(values, count):
    if count == 2:
        return [values[0] + values[1], values[0] - values[1]]
    split = count // 4 + 1
    even, odd = even_points(values[:split], count // 2), odd_points(values[split:])
    return [a + b for a, b in zip(even, odd)] + [a - b for a, b in zip(even, odd)]


def short_values(points):
    return even_values(points) + odd_values(points)


def short_points(values, count):
    split = count // 2 + 1
    even, odd = even_points(values[:split], count), odd_points(values[split:])
    return [a + b for a, b in zip(even, odd)]


def short_angles(count):
    zero = [(0.0, 0.0)] * count
    odd = lambda n: [angle for angle, *_ in evaluate(zero[: n // 2], math.pi / 2)]
    sizes, even = [count], count
    while even > 2:
        even //= 2
        sizes.append(even)
    return [0.0, math.pi] + sum((odd(n) for n in reversed(sizes)), [])


def make_tables(count, width, tile):
    angles = np.array(short_angles(count))
    turn = np.outer(angles, np.arange(width)) / width
    scale = np.where(np.arange(len(angles)) < 2, 1.0, 2.0)[:, None] / (2 * count * width)
    twist = np.stack(
        [np.cos(turn), np.sin(turn), np.cos(turn) * scale, np.sin(turn) * scale], axis=1
    ).astype(np.float32)
    wave = np.outer(np.arange(width), np.arange(width)) % width * (2 * math.pi / width)
    c, s = np.cos(wave), np.sin(wave)
    ahead = np.block([[c, -s], [s, c]])
    short = back = np.zeros((2, 1, 1))
    if on_matrix_unit(count, tile):
        turn = np.outer(angles, np.arange(count))
        parts = np.stack([np.cos(turn), -np.sin(turn)], axis=1)
        parts = np.concatenate([parts[:2, 0], parts[2:].reshape(-1, count)])
        size = count * tile
        short = np.kron(parts, np.eye(tile)).reshape(2, size, size)
        scale = np.where(np.arange(2 * count) < 2, 1.0, 2.0)[:, None] / (2 * size // tile * width)
        back = np.kron((parts * scale).T, np.eye(tile)).reshape(size, 2, size).swapaxes(0, 1)
    waves = np.stack([ahead, ahead.T])
    return (twist, *(jnp.asarray(table, jnp.bfloat16) for table in (waves, short, back)))


def on_matrix_unit(count, tile):
    return count * tile <= 256


def rows_of(block, chunk):
    return pl.ds(pl.multiple_of(block * chunk, chunk), chunk)


def gate_kernel(value_hbm, key_hbm, cot_hbm, query_hbm, out_hbm, *scratch):
    blocks, _, chunk, width = out_hbm.shape
    sources = (value_hbm, key_hbm, cot_hbm, query_hbm)
    *held, made, loads, stores = scratch
    span, some = blocks * chunk // STEPS, blocks // STEPS
    copies = []
    for step in range(STEPS):
        rows = pl.ds(step * span, span)
        copies.append(
            [
                pltpu.make_async_copy(source.at[rows], to.at[rows], loads.at[i, step])
                for i, (source, to) in enumerate(zip(sources, held))
            ]
        )
        for copy in copies[-1]:
            copy.start()
    sends = []
    for step in range(STEPS):
        for copy in copies[step]:
            copy.wait()
        rows, part = pl.ds(step * span, span), pl.ds(step * some, some)
        for which in range(2):
            left, right = held[2 * which][rows], held[2 * which + 1][rows]
            both = left.astype(jnp.float32) * right.astype(jnp.float32)
            made[part, which] = both.astype(jnp.bfloat16).reshape(some, chunk, width)
        sends.append(pltpu.make_async_copy(made.at[part], out_hbm.at[part], stores.at[step]))
        sends[-1].start()
    for send in sends:
        send.wait()


def short_stage(blocks, short_ref):
    count, (tile, width) = len(blocks[0]), blocks[0][0].shape
    if not on_matrix_unit(count, tile):
        blocks = [[b.astype(jnp.float32) for b in points] for points in blocks]
        values = [short_values(points) for points in blocks]
        return [v[:2] + [(re, im) for _, re, im in v[2:]] for v in values]
    side = jnp.concatenate([jnp.concatenate(points) for points in blocks], axis=1)
    parts = jnp.concatenate(
        [jnp.dot(short_ref[i], side, preferred_element_type=jnp.float32) for i in range(2)]
    )

    def part(i, which):
        return parts[i * tile : (i + 1) * tile, which * width : (which + 1) * width]

    return [
        [part(0, which), part(1, which)]
        + [(part(2 * k - 2, which), part(2 * k - 1, which)) for k in range(2, count + 1)]
        for which in range(len(blocks))
    ]


def transform(blocks, twist_ref, wave_ref, short_ref, turned_ref):
    tile, width = blocks[0][0].shape
    tall = (len(blocks[0]) + 1) * tile
    for which, values in enumerate(short_stage(blocks, short_ref)):
        for k, value in enumerate(values):
            c, s = twist_ref[k, 0:1, :], twist_ref[k, 1:2, :]
            if k == 0:
                re, im = value, jnp.zeros_like(value)
            elif k == 1:
                re, im = value * c, value * -s
            else:
                re, im = value[0] * c + value[1] * s, value[1] * c - value[0] * s
            rows = slice(which * tall + k * tile, which * tall + (k + 1) * tile)
            turned_ref[rows, :width] = re.astype(jnp.bfloat16)
            turned_ref[rows, width:] = im.astype(jnp.bfloat16)
    turned = turned_ref[: len(blocks) * tall]
    spec = jnp.dot(turned, wave_ref[0], preferred_element_type=jnp.float32)
    return [spec[which * tall : (which + 1) * tall] for which in range(len(blocks))]


def inverse(re, im, twist_ref, wave_ref):
    count, _, width = twist_ref.shape
    tile = re.shape[0] // count
    both = jnp.concatenate([re.astype(jnp.bfloat16), im.astype(jnp.bfloat16)], axis=1)
    back = jnp.dot(both, wave_ref[1], preferred_element_type=jnp.float32)
    parts = []
    for start in range(0, tile, 8):
        values = []
        for k in range(count):
            rows = slice(k * tile + start, k * tile + start + 8)
            re, im = back[rows, :width], back[rows, width:]
            c, s = twist_ref[k, 2:3, :], twist_ref[k, 3:4, :]
            if k == 0:
                values.append(re * c)
            elif k == 1:
                values.append(re * c - im * s)
            else:
                values.append((re * c - im * s, re * s + im * c))
        parts.append(short_points(values, count - 1))
    return [jnp.concatenate(part) for part in zip(*parts)]


def held_inverse(re, im, twist_ref, wave_ref, held_ref):
    count, _, width = twist_ref.shape
    tile = re.shape[0] // count
    both = jnp.concatenate([re.astype(jnp.bfloat16), im.astype(jnp.bfloat16)], axis=1)
    back = jnp.dot(both, wave_ref[1], preferred_element_type=jnp.float32)
    for k in range(count):
        rows = slice(k * tile, (k + 1) * tile)
        re, im = back[rows, :width], back[rows, width:]
        c, s = twist_ref[k, 0:1, :], twist_ref[k, 1:2, :]
        first = k if k < 2 else 2 * k - 2
        held_ref[first * tile : (first + 1) * tile] = (re * c - im * s).astype(jnp.bfloat16)
        if k > 1:
            rows = slice((first + 1) * tile, (first + 2) * tile)
            held_ref[rows] = (re * s + im * c).astype(jnp.bfloat16)


def filter_kernel(mine_ref, other_ref, twist_ref, wave_ref, short_ref, spec_ref, turned_ref):
    near, far, rows, _ = mine_ref.shape
    tile = spec_ref.shape[1] // twist_ref.shape[0]
    me, side = lax.axis_index("ctx"), lax.axis_index("groups")
    for first, table in ((4, wave_ref), (2, short_ref)):
        for i in range(table.shape[0]):
            _, high, wide = table.shape
            spec_ref[spec_ref.shape[0] - first + i, :high, :wide] = table[i]

    def piece(share_ref, b, lanes):
        return share_ref[(me % near) ^ (b % near), (me // near) ^ (b // near), lanes]

    def points(first, lanes):
        return [
            jnp.where(side == first, piece(mine_ref, b, lanes), piece(other_ref, b, lanes))
            for b in range(near * far)
        ]

    if rows < tile:
        parts = zip(*[points(half, slice(None)) for half in range(2)])
        joined = [jnp.concatenate([p.astype(jnp.float32) for p in pair]) for pair in parts]
        (spec,) = transform([joined], twist_ref, wave_ref, short_ref, turned_ref)
        spec_ref[0] = spec.astype(jnp.bfloat16)
        return
    group = turned_ref.shape[0] // spec_ref.shape[1] // 2

    @pl.loop(0, rows // tile // group)
    def _(step):
        tiles = [step * group + t for t in range(group)]
        blocks = [points(half, rows_of(t, tile)) for half in range(2) for t in tiles]
        specs = transform(blocks, twist_ref, wave_ref, short_ref, turned_ref)
        for i, spec in enumerate(specs):
            half, t = i // group, tiles[i % group]
            spec_ref[half * (rows // tile) + t] = spec.astype(jnp.bfloat16)


def spectral_kernel(sig_ref, spec_ref, twist_ref, back_hbm, *refs):
    *out_refs, made_ref, turned_ref, held_ref, back_ref, back_sem = refs
    count, _, chunk, width = sig_ref.shape
    tile = spec_ref.shape[1] // twist_ref.shape[0]
    group = turned_ref.shape[0] // spec_ref.shape[1] // 2
    me, steps = lax.axis_index("ctx"), chunk // tile // group
    size = count * tile if on_matrix_unit(count, tile) else 1
    wave_ref = spec_ref.at[chunk // tile : chunk // tile + 2, : 2 * width]
    short_ref = spec_ref.at[chunk // tile + 2 :, :size, :size]

    on_unit = ON_UNIT if on_matrix_unit(count, tile) else 0
    fetch = pltpu.make_async_copy(back_hbm, back_ref, back_sem)
    fetch.start()

    def deliver(step):
        lanes = rows_of(step, tile * group)
        for k in range(count):
            out_refs[k][:, lanes] = made_ref[k, :, lanes]

    for step in range(steps):
        if step:
            deliver(step - 1)
        tiles = [step * group + t for t in range(group)]
        blocks = [
            [sig_ref[b, which, rows_of(t, tile)] for b in range(count)]
            for t in tiles
            for which in range(2)
        ]
        both = transform(blocks, twist_ref, wave_ref, short_ref, turned_ref)
        for i, t in enumerate(tiles):
            specs = [*both[2 * i : 2 * i + 2], spec_ref[t].astype(jnp.float32)]
            (m_re, m_im), (g_re, g_im), (f_re, f_im) = ((s[:, :width], s[:, width:]) for s in specs)
            results = (
                (f_re * m_re - f_im * m_im, f_re * m_im + f_im * m_re),
                (f_re * g_re + f_im * g_im, f_re * g_im - f_im * g_re),
                (g_re * m_re + g_im * m_im, g_im * m_re - g_re * m_im),
            )
            for which, (re, im) in enumerate(results):
                if which >= 3 - on_unit:
                    lanes = slice(i * width, (i + 1) * width)
                    held_inverse(re, im, twist_ref, wave_ref, held_ref.at[which + on_unit - 3, :, lanes])
                    continue
                for b, part in enumerate(inverse(re, im, twist_ref, wave_ref)):
                    made_ref[me ^ b, which, rows_of(t, tile)] = part.astype(jnp.bfloat16)
        if step == 0:
            fetch.wait()
        for n in range(on_unit):
            points = sum(
                jnp.dot(
                    back_ref[h],
                    held_ref[n, h * size : (h + 1) * size],
                    preferred_element_type=jnp.float32,
                )
                for h in range(2)
            ).astype(jnp.bfloat16)
            for i, t in enumerate(tiles):
                for b in range(count):
                    part = points[b * tile : (b + 1) * tile, i * width : (i + 1) * width]
                    made_ref[me ^ b, 3 - on_unit + n, rows_of(t, tile)] = part

    deliver(steps - 1)


def gates(operands, part_ref, made, rows):
    value, key, cot = (operand.astype(jnp.float32) for operand in operands)
    conv, grad, filt = (part_ref[which].astype(jnp.float32) for which in range(3))
    made[0][rows] = (grad * key).astype(jnp.bfloat16)
    made[1][rows] = (grad * value).astype(jnp.bfloat16)
    made[2][rows] = (cot * conv).astype(jnp.bfloat16)
    made[3][rows] = filt


def send_rows(made, outs, rows, sems, i):
    sends = [
        pltpu.make_async_copy(source.at[rows], to.at[rows], sems.at[j, i])
        for j, (source, to) in enumerate(zip(made, outs))
    ]
    for send in sends:
        send.start()
    return sends


def first_gates(early, late, *refs):
    operands, part_refs = refs[:3], refs[3 : 3 + len(early)]
    *outs, late_ref = refs[3 + len(early) : 8 + len(early)]
    held_ref, *made, loads, stores = refs[8 + len(early) :]
    me = lax.axis_index("ctx")
    copies = []
    for i, k in enumerate(early + late):
        rows = rows_of(me ^ k, part_refs[0].shape[1])
        to = held_ref.at[i] if i < len(early) else late_ref.at[i - len(early)]
        copies.append(
            [
                pltpu.make_async_copy(operand.at[rows], to.at[j], loads.at[j, i])
                for j, operand in enumerate(operands)
            ]
        )
        for copy in copies[-1]:
            copy.start()
    sends = []
    for i, k in enumerate(early):
        for copy in copies[i]:
            copy.wait()
        rows = rows_of(me ^ k, part_refs[0].shape[1])
        gates([held_ref[i, j] for j in range(3)], part_refs[i], made, rows)
        sends += send_rows(made, outs, rows, stores, i)
    for copy in sum(copies[len(early) :], []) + sends:
        copy.wait()


def last_gates(late, held_ref, *refs):
    part_refs, outs = refs[: len(late)], refs[len(late) + 4 : len(late) + 8]
    *made, stores = refs[len(late) + 8 :]
    me = lax.axis_index("ctx")
    sends = []
    for i, k in enumerate(late):
        rows = rows_of(me ^ k, part_refs[0].shape[1])
        gates([held_ref[i, j] for j in range(3)], part_refs[i], made, rows)
        sends += send_rows(made, outs, rows, stores, i)
    for send in sends:
        send.wait()


def partners(count):
    near, size = [], count // 4
    while size:
        near += range(size, 2 * size)
        size //= 2
    far = list(range(count // 2, count))
    order = []
    for i, k in enumerate(far):
        order += [k] + near[i : i + 1]
    return order


def spread(blocks):
    count = len(blocks)
    got = list(blocks)
    order = partners(count)
    for i, k in enumerate(order):
        block = blocks[k]
        if i >= WINDOW:
            before = order[i - WINDOW]
            block, got[before] = lax.optimization_barrier((block, got[before]))
        got[k] = lax.ppermute(block, "ctx", [(j, j ^ k) for j in range(count)])
    return got


def exchange(parts):
    return lax.all_to_all(parts, "ctx", split_axis=0, concat_axis=0, tiled=True)


def swap(block, axis, gap):
    size = lax.axis_size(axis)
    return lax.ppermute(block, axis, [(i, i ^ gap) for i in range(size)])


def pick(blocks, where):
    return lax.dynamic_index_in_dim(blocks, where, 0, keepdims=False)


def far_filters(filters, far):
    count, me, side = lax.axis_size("ctx"), lax.axis_index("ctx"), lax.axis_index("groups")
    near = count // far
    channels, width = filters.shape
    share = filters.reshape(far, near, 2, channels // count // 2, width)
    share = lax.dynamic_index_in_dim(share, side, 2, keepdims=False)
    blocks = [pick(share, (me // near) ^ k).astype(jnp.bfloat16) for k in range(far)]
    return blocks[:1] + [swap(blocks[k], "ctx", k * near) for k in range(1, far)]


def near_filters(blocks):
    me, near = lax.axis_index("ctx"), blocks[0].shape[0]
    parts = [jnp.stack([pick(b, (me % near) ^ j) for b in blocks]) for j in range(near)]
    mine = jnp.stack(parts[:1] + [swap(parts[j], "ctx", j) for j in range(1, near)])
    return mine, swap(mine, "groups", 1)


def shards(values, keys, queries, grad_out, filters):
    count = lax.axis_size("ctx")
    channels, width = values.shape
    chunk = channels // count
    tile = min(TILE, chunk)
    twist, wave, short, back = make_tables(count, width, tile)
    here = pl.BlockSpec(memory_space=pltpu.VMEM)
    limit = pltpu.CompilerParams(vmem_limit_bytes=24 * 1024 * 1024)
    far = 1 << ((count.bit_length() - 1) // 2)
    blocks = far_filters(filters, far)
    hbm = pl.BlockSpec(memory_space=pl.ANY)
    sent = pl.pallas_call(
        gate_kernel,
        in_specs=[hbm] * 4,
        out_specs=hbm,
        out_shape=jax.ShapeDtypeStruct((count, 2, chunk, width), jnp.bfloat16),
        scratch_shapes=[pltpu.VMEM((channels, width), jnp.bfloat16)] * 4
        + [
            pltpu.VMEM((count, 2, chunk, width), jnp.bfloat16),
            pltpu.SemaphoreType.DMA((4, STEPS)),
            pltpu.SemaphoreType.DMA((STEPS,)),
        ],
    )(values, keys, grad_out, queries)
    blocks, sent = lax.optimization_barrier((blocks, sent))
    held = exchange(sent)
    mine, other = near_filters(blocks)
    group = min(GROUP, chunk // tile)
    tall = (count + 1) * tile
    spec = pl.pallas_call(
        filter_kernel,
        in_specs=[here] * 5,
        out_specs=here,
        out_shape=jax.ShapeDtypeStruct((chunk // tile + 4, tall, 2 * width), jnp.bfloat16),
        scratch_shapes=[pltpu.VMEM((2 * max(group // 2, 1) * tall, 2 * width), jnp.bfloat16)],
        compiler_params=limit,
        cost_estimate=pl.CostEstimate(
            flops=8 * count * chunk * width * width, bytes_accessed=2**20, transcendentals=0
        ),
    )(mine, other, twist, wave, short)
    message = jax.ShapeDtypeStruct((3, chunk, width), jnp.bfloat16)
    made = pl.pallas_call(
        spectral_kernel,
        in_specs=[here] * 3 + [hbm],
        out_specs=[here] * count,
        out_shape=[message] * count,
        scratch_shapes=[
            pltpu.VMEM((count, 3, chunk, width), jnp.bfloat16),
            pltpu.VMEM((2 * group * tall, 2 * width), jnp.bfloat16),
            pltpu.VMEM((ON_UNIT, 2 * count * tile, group * width), jnp.bfloat16),
            pltpu.VMEM(back.shape, jnp.bfloat16),
            pltpu.SemaphoreType.DMA,
        ],
        compiler_params=limit,
    )(held, spec, twist, back)
    got = spread(made)
    half = jax.ShapeDtypeStruct((channels, width), jnp.bfloat16)
    wide = jax.ShapeDtypeStruct((channels, width), jnp.float32)
    order = [0] + partners(count)
    early, late = order[:-LATE], order[-LATE:]
    made_scratch = [pltpu.VMEM((channels, width), jnp.bfloat16)] * 3 + [
        pltpu.VMEM((channels, width), jnp.float32)
    ]
    *outs, operands = pl.pallas_call(
        functools.partial(first_gates, early, late),
        in_specs=[hbm] * 3 + [here] * len(early),
        out_specs=[hbm] * 4 + [here],
        out_shape=[half] * 3
        + [wide, jax.ShapeDtypeStruct((len(late), 3, chunk, width), jnp.bfloat16)],
        scratch_shapes=[
            pltpu.VMEM((len(early), 3, chunk, width), jnp.bfloat16),
            *made_scratch,
            pltpu.SemaphoreType.DMA((3, count)),
            pltpu.SemaphoreType.DMA((4, len(early))),
        ],
        compiler_params=pltpu.CompilerParams(vmem_limit_bytes=24 * 1024 * 1024),
    )(values, keys, grad_out, *[got[k] for k in early])
    return pl.pallas_call(
        functools.partial(last_gates, late),
        in_specs=[here] * (1 + len(late)) + [hbm] * 4,
        out_specs=[hbm] * 4,
        out_shape=[half] * 3 + [wide],
        input_output_aliases={1 + len(late) + i: i for i in range(4)},
        scratch_shapes=[*made_scratch, pltpu.SemaphoreType.DMA((4, len(late)))],
        compiler_params=limit,
    )(operands, *[got[k] for k in late], *outs)


def solution(mesh):
    token = P(None, ("groups", "ctx"))
    return jax.shard_map(
        shards,
        mesh=mesh,
        in_specs=(token, token, token, token, P(None, "ctx")),
        out_specs=(token, token, token, token),
        check_vma=False,
    )
```
